256 devices in a mesh: seq: 32 (over y, z), mp: 8 (over x, core).
Axes of the slice: x: 4, y: 4, z: 8, core: 2. Of those that a mesh axis runs over, the one named last changes fastest.
Arguments:
- queries: bfloat16 [16384, 4096], P('seq', 'mp'), may hold values from -30 to 30
- keys: bfloat16 [16384, 1024], P('seq', 'mp'), may hold values from -6 to 6
- values: bfloat16 [16384, 1024], P('seq', 'mp'), may hold values from -6 to 6
- routing: int32 [32, 32, 3], P(None, 'mp'), may hold values from 0 to 31, as said below
- w_out: bfloat16 [4096, 4096], P('mp', 'seq'), may hold values from -0.09375 to 0.09375
Outputs:
- mixed: bfloat16 [16384, 4096], P('seq', 'mp')
The draws below stay inside these ranges and needn't reach their ends.
Inputs may be any that keep to these rules, and one draw needn't show every extreme that they name: `routing`: entries of one query block i and head are distinct where below i; they are min(i, 3) distinct blocks before i, and any other entry equals i.
All inputs are finite; a program needn't handle non-finite values.
Results may differ from the reference program's by a relative error of at most 0.02.
Values may be sent and summed in bfloat16 or wider, within the bound.
No kernel may reach another device: no remote copies, remote signals or barrier semaphores. Data moves between devices by JAX's collectives and lax.ppermute only.
A program may use at most 128 MiB of HBM per device.

```python
import math
import jax
import jax.numpy as jnp
from jax import lax

D = 4096
H = 32
KVH = 8
HD = 128
BLK = 512
TOPK = 3
NB = 32
TOKENS = 16384
N_MP = 8


def draw_queries(key, part):
    key = jax.random.fold_in(key, 11)
    result = jnp.clip(jax.random.normal(key, (TOKENS, H * HD), jnp.float32), -6.0, 6.0)
    return result.astype(jnp.bfloat16)


def draw_keys(key, part):
    key = jax.random.fold_in(key, 12)
    result = jnp.clip(jax.random.normal(key, (TOKENS, KVH * HD), jnp.float32), -6.0, 6.0)
    return result.astype(jnp.bfloat16)


def draw_routing(key, part):
    key = jax.random.fold_in(key, 5)
    key_hot, key_noise = jax.random.split(key)
    hot = jax.random.randint(key_hot, (NB,), 0, 4) * 256
    noise = jax.random.randint(key_noise, (NB, H, NB), 0, 1024)
    blocks = jnp.arange(NB)
    score = (noise + hot[None, None, :]) * NB + blocks[None, None, :]
    earlier = blocks[None, None, :] < blocks[:, None, None]
    score = jnp.where(earlier, score, -1 - blocks[None, None, :])
    top_vals, top_idx = jax.lax.top_k(score, TOPK)
    route = jnp.where(top_vals >= 0, top_idx, blocks[:, None, None])
    return route.astype(jnp.int32)


def steps_of(own_key, dims, shards, smallest, high):
    factor_of = 1.0
    for dim, blocks in shards:
        steps = jax.random.uniform(jax.random.fold_in(jax.random.fold_in(own_key, 6), dim), (blocks,), jnp.float32, smallest / len(shards), high / len(shards))
        factor_of = factor_of * jnp.repeat(jnp.exp(steps), dims[dim] // blocks).reshape((-1,) + (1,) * (len(dims) - 1 - dim))
    return factor_of


def bell_draw(own_key, shape, scale, most, pieces=(), dtype=jnp.bfloat16):
    values = scale * jax.random.normal(own_key, shape, jnp.float32)
    if pieces:
        values = values * steps_of(own_key, shape, pieces, -0.22, 0.18)
    return jnp.clip(values, -most, most).astype(dtype)


def setup_inputs(seed: int = 0) -> dict:
    key_of = jax.random.split(jax.random.key(seed), 6)
    return {
        "queries": draw_queries(jax.random.fold_in(key_of[5], 71), 0),
        "keys": draw_keys(jax.random.fold_in(key_of[5], 71), 0),
        "values": bell_draw(key_of[2], (TOKENS, KVH * HD), 1.0, 6.0, ((0, 32), (1, 8))),
        "routing": draw_routing(jax.random.fold_in(key_of[5], 71), 0),
        "w_out": bell_draw(key_of[4], (H * HD, D), (H * HD) ** -0.5, 0.09375, ((0, 8), (1, 32))),
    }


def attend(q, k, v, allowed):
    scale = 1.0 / math.sqrt(HD)
    s = jnp.einsum('hqd,hkd->hqk', q.astype(jnp.float32), k.astype(jnp.float32)) * scale
    if allowed is not None:
        s = jnp.where(allowed, s, -1e+30)
    m = lax.optimization_barrier(jnp.max(s, axis=-1))
    e = jnp.exp(s - m[..., None])
    if allowed is not None:
        e = jnp.where(allowed, e, 0.0)
    l = lax.optimization_barrier(jnp.sum(e, axis=-1))
    o = jnp.einsum('hqk,hkd->hqd', e.astype(jnp.bfloat16).astype(jnp.float32), v.astype(jnp.float32))
    return ((o / l[..., None]).astype(jnp.bfloat16), m + jnp.log(l))

def reference(queries, keys, values, routing, w_out):
    group = H // KVH
    kv_of = jnp.arange(H) // group
    qb = queries.reshape(NB, BLK, H, HD)
    kb = keys.reshape(NB, BLK, KVH, HD)
    vb = values.reshape(NB, BLK, KVH, HD)
    pos = jnp.arange(BLK)
    causal = pos[:, None] >= pos[None, :]

    def one_block(i):
        q = jnp.transpose(qb[i], (1, 0, 2))
        k_own = jnp.transpose(kb[i][:, kv_of], (1, 0, 2))
        v_own = jnp.transpose(vb[i][:, kv_of], (1, 0, 2))
        part, lse = attend(q, k_own, v_own, causal)
        parts = [part.astype(jnp.float32)]
        lses = [lse]
        for s in range(TOPK):
            j = routing[i, :, s].astype(jnp.int32)
            k_sel = kb[j, :, kv_of]
            v_sel = vb[j, :, kv_of]
            part, lse = attend(q, k_sel, v_sel, None)
            lse = jnp.where((j < i)[:, None], lse, -1e+30)
            parts.append(part.astype(jnp.float32))
            lses.append(lse)
        stacked = jnp.stack(lses)
        top = lax.optimization_barrier(jnp.max(stacked, axis=0))
        wts = jnp.exp(stacked - top[None])
        total = lax.optimization_barrier(jnp.sum(wts[..., None] * jnp.stack(parts), axis=0)) / lax.optimization_barrier(jnp.sum(wts, axis=0))[..., None]
        return jnp.transpose(total.astype(jnp.bfloat16), (1, 0, 2)).reshape(BLK, H * HD)
    attn = lax.map(one_block, jnp.arange(NB)).reshape(TOKENS, H * HD)
    width = H * HD // N_MP
    summed = jnp.zeros((TOKENS, D), jnp.float32)
    for g in range(N_MP):
        partial_value = jnp.dot(attn[:, g * width:(g + 1) * width], w_out[g * width:(g + 1) * width], preferred_element_type=jnp.float32).astype(jnp.bfloat16)
        partial_value = lax.optimization_barrier(partial_value)
        summed = summed + partial_value.astype(jnp.float32)
    return summed.astype(jnp.bfloat16)
```

```python
import functools
import math

import jax
import jax.numpy as jnp
from jax import lax
from jax.experimental import pallas as pl
from jax.experimental.pallas import tpu as pltpu
from jax.sharding import Mesh, PartitionSpec as P

HD = 128
BLK = 512
HEADS = 4
SLOTS = 3
NY, NZ, NX, NC = 4, 8, 4, 2
AXES = ("y", "z", "x", "c")
ZROWS = 304
YROWS = BLK - ZROWS
SCALE = math.log2(math.e) / math.sqrt(HD)
Z_STACK = {0: (0, 0), 1: (0, 1), 7: (0, 2), 2: (0, 3), 6: (1, 0), 3: (1, 1), 5: (1, 2), 4: (1, 3)}
Y_CODE = {0: 0, 3: 1, 1: 2, 2: 3}


def shift(v, axis, d, n):
    return lax.ppermute(v, axis, [(i, (i + d) % n) for i in range(n)])


zp = functools.partial(shift, axis="z", d=1, n=NZ)
zm = functools.partial(shift, axis="z", d=-1, n=NZ)
yp = functools.partial(shift, axis="y", d=1, n=NY)
ym = functools.partial(shift, axis="y", d=-1, n=NY)
xp = functools.partial(shift, axis="x", d=1, n=NX)
xm = functools.partial(shift, axis="x", d=-1, n=NX)
swap = functools.partial(shift, axis="c", d=1, n=NC)


def gate(vals, waits):
    return lax.optimization_barrier((vals, waits))


def gather_kv(kv):
    zc, yc = kv[:ZROWS], kv[ZROWS:]
    hz, hy = ZROWS // 2, YROWS // 2
    y1p, y1m, z1p, z1m = yp(yc), ym(yc), zp(zc), zm(zc)
    (y1p, y1m, z1p, z1m), _ = gate((y1p, y1m, z1p, z1m), ())
    y2p, y2m, z2p, z2m = yp(y1p[:hy]), ym(y1m[hy:]), zp(z1p), zm(z1m)
    s0 = jnp.stack([yc, y1p, y1m, jnp.concatenate([y2p, y2m])])
    a1p, a1m = zp(s0), zm(s0)
    z3p, z3m = zp(z2p), zm(z2m)
    g1 = jnp.stack([zc, z1m, z1p, z2m])
    g1p, g1m = yp(g1), ym(g1)
    (a1p, a1m), (z3p, z3m) = gate((a1p, a1m), (z3p, z3m))
    z4p, z4m = zp(z3p[:hz]), zm(z3m[hz:])
    a2p, a2m = zp(a1p), zm(a1m)
    g2 = jnp.stack([z2p, z3m, z3p, jnp.concatenate([z4p, z4m])])
    (g1p, g1m), g2 = gate((g1p, g1m), g2)
    g1h, g1l = yp(g1p[:2]), ym(g1m[2:])
    g2p, g2m = yp(g2), ym(g2)
    a3p, a3m = zp(a2p), zm(a2m)
    g2h, g2l = yp(g2p[:2]), ym(g2m[2:])
    a4p, a4m = zp(a3p[:2]), zm(a3m[2:])
    za = [g1, g1p, g1m, jnp.concatenate([g1h, g1l]), g2, g2p, g2m, jnp.concatenate([g2h, g2l])]
    ya = [s0, a1m, a2m, a3m, jnp.concatenate([a4p, a4m]), a3p, a2p, a1p]
    return za, ya


def block_places(route, y, z):
    me = y * NZ + z
    dy, dz = (route // NZ - y) % NY, (route % NZ - z) % NZ
    pick = lambda table, i: jnp.asarray(table, jnp.int32)[i]
    ycode = pick([Y_CODE[i] for i in range(NY)], dy)
    group = pick([Z_STACK[i][0] for i in range(NZ)], dz)
    slot = pick([Z_STACK[i][1] for i in range(NZ)], dz)
    ok = (route < me).astype(jnp.int32)
    return jnp.stack([group * 4 + ycode, slot, dz, ycode, ok]).reshape(-1)


TILE = 128


def own_kernel(q_ref, kv_ref, m_ref, l_ref, o_ref):
    for h in range(HEADS):
        cols = slice(h * HD, (h + 1) * HD)
        for t in range(BLK // TILE):
            rows = slice(t * TILE, (t + 1) * TILE)
            n = (t + 1) * TILE
            s = lax.dot_general(
                q_ref[rows, cols], kv_ref[:n, :HD], (((1,), (1,)), ((), ())), preferred_element_type=jnp.float32
            )
            qpos = t * TILE + lax.broadcasted_iota(jnp.int32, (TILE, n), 0)
            s = jnp.where(qpos >= lax.broadcasted_iota(jnp.int32, (TILE, n), 1), s * SCALE, -1e30)
            m = jnp.max(s, axis=1, keepdims=True)
            e = jnp.exp2(s - m)
            m_ref[h, rows, :] = jnp.broadcast_to(m, (TILE, HD))
            l_ref[h, rows, :] = jnp.broadcast_to(jnp.sum(e, axis=1, keepdims=True), (TILE, HD))
            o_ref[rows, cols] = jnp.dot(e.astype(jnp.bfloat16), kv_ref[:n, HD:], preferred_element_type=jnp.float32)


def routed_kernel(place_ref, q_ref, m_ref, l_ref, o_ref, *rest):
    za, ya, out_ref, buf, sems = rest[:8], rest[8:16], rest[16], rest[17], rest[18]
    n = HEADS * SLOTS

    def copies(u, act):
        for a in range(8):

            @pl.when(place_ref[u] == a)
            def _():
                act(pltpu.make_async_copy(za[a].at[place_ref[n + u]], buf.at[u, pl.ds(0, ZROWS)], sems.at[u, 0]))

            @pl.when(place_ref[2 * n + u] == a)
            def _():
                act(pltpu.make_async_copy(ya[a].at[place_ref[3 * n + u]], buf.at[u, pl.ds(ZROWS, YROWS)], sems.at[u, 1]))

    for u in range(n):
        copies(u, lambda c: c.start())
    for h in range(HEADS):
        cols = slice(h * HD, (h + 1) * HD)
        for s in range(SLOTS):
            u = h * SLOTS + s
            pltpu.make_async_copy(za[0].at[0], buf.at[u, pl.ds(0, ZROWS)], sems.at[u, 0]).wait()
            pltpu.make_async_copy(ya[0].at[0], buf.at[u, pl.ds(ZROWS, YROWS)], sems.at[u, 1]).wait()
        for t in range(BLK // TILE):
            rows = slice(t * TILE, (t + 1) * TILE)
            scores = []
            m0 = m_ref[h, rows, :1]
            m = m0
            for s in range(SLOTS):
                u = h * SLOTS + s
                sc = lax.dot_general(
                    q_ref[rows, cols], buf[u, :, :HD], (((1,), (1,)), ((), ())), preferred_element_type=jnp.float32
                )
                sc = jnp.where(place_ref[4 * n + u] == 1, sc * SCALE, -1e30)
                m = jnp.maximum(m, jnp.max(sc, axis=1, keepdims=True))
                scores.append(sc)
            w0 = jnp.exp2(m0 - m)
            l = l_ref[h, rows, :1] * w0
            acc = o_ref[rows, cols] * w0
            for s in range(SLOTS):
                e = jnp.exp2(scores[s] - m)
                l = l + jnp.sum(e, axis=1, keepdims=True)
                acc = acc + jnp.dot(e.astype(jnp.bfloat16), buf[h * SLOTS + s, :, HD:], preferred_element_type=jnp.float32)
            out_ref[rows, cols] = (acc / l).astype(out_ref.dtype)


def attention_own(q, kv):
    stat = jax.ShapeDtypeStruct((HEADS, BLK, HD), jnp.float32)
    return pl.pallas_call(
        own_kernel,
        out_shape=(stat, stat, jax.ShapeDtypeStruct((BLK, HEADS * HD), jnp.float32)),
        compiler_params=pltpu.CompilerParams(vmem_limit_bytes=32 << 20),
    )(q, kv)


def attention_routed(places, q, m, l, o, za, ya):
    n = HEADS * SLOTS
    vmem = pl.BlockSpec(memory_space=pltpu.VMEM)
    return pl.pallas_call(
        routed_kernel,
        out_shape=jax.ShapeDtypeStruct((BLK, HEADS * HD), jnp.bfloat16),
        in_specs=[pl.BlockSpec(memory_space=pltpu.SMEM)] + [vmem] * 4 + [pl.BlockSpec(memory_space=pl.ANY)] * 16,
        out_specs=vmem,
        scratch_shapes=[pltpu.VMEM((n, BLK, 2 * HD), jnp.bfloat16), pltpu.SemaphoreType.DMA((n, 2))],
        compiler_params=pltpu.CompilerParams(vmem_limit_bytes=32 << 20),
    )(places, q, m, l, o, *za, *ya)


def body(queries, keys, values, routing, w_out):
    y, z, x, c = (lax.axis_index(a) for a in AXES)
    kv = jnp.concatenate([keys, values], axis=1)
    at = lambda y, z, x, c: ((y * NZ + z) * NX + x) * NC + c
    turn = [
        (at(y, z, x, c), at(x, z, y, c)) for y in range(NY) for z in range(NZ) for x in range(NX) for c in range(NC)
    ]
    w = lax.ppermute(w_out, AXES, turn)
    w_all = lax.all_gather(w, ("y", "z"), axis=0, tiled=False)
    route = lax.dynamic_index_in_dim(routing, y * NZ + z, 0, keepdims=False)
    places = block_places(route.reshape(-1), y, z)
    m, l, o = attention_own(queries, kv)
    za, ya = gather_kv(kv)
    attn = attention_routed(places, queries, m, l, o, za, ya)
    x1p, x1m = xp(attn), xm(attn)
    x2p, x2m = xp(x1p[: BLK // 2]), xm(x1m[BLK // 2 :])
    w_rows = w_all.reshape(NY, NZ, BLK, HD)

    def product(a, dx):
        rows = lax.dynamic_index_in_dim(w_rows, (x + dx) % NX, 0, keepdims=False)
        rows = jnp.transpose(rows, (1, 0, 2)).reshape(BLK, NZ * HD)
        return jnp.dot(a, rows, preferred_element_type=jnp.float32)

    total = product(attn, 0) + product(x1p, -1) + product(x1m, 1)
    total = total + product(jnp.concatenate([x2p, x2m]), 2)
    half = NZ * HD // NC
    mine = lax.dynamic_slice_in_dim(total, c * half, half, 1)
    other = lax.dynamic_slice_in_dim(total, (1 - c) * half, half, 1)
    theirs = swap(other.astype(jnp.bfloat16))
    return (mine + theirs.astype(jnp.float32)).astype(jnp.bfloat16)


def solution(mesh):
    grid = Mesh(mesh.devices.reshape(NY, NZ, NX, NC), AXES)
    seq, mp = ("y", "z"), ("x", "c")
    in_specs = (P(seq, mp), P(seq, mp), P(seq, mp), P(None, mp, None), P(mp, seq))
    return jax.shard_map(body, mesh=grid, in_specs=in_specs, out_specs=P(seq, mp), check_vma=False)
```

```python
import functools
import math

import jax
import jax.numpy as jnp
from jax import lax
from jax.experimental import pallas as pl
from jax.experimental.pallas import tpu as pltpu
from jax.sharding import Mesh, PartitionSpec as P

HD = 128
BLK = 512
HEADS = 4
SLOTS = 3
NY, NZ, NX, NC = 4, 8, 4, 2
AXES = ("y", "z", "x", "c")
ZROWS = 304
YROWS = BLK - ZROWS
SCALE = math.log2(math.e) / math.sqrt(HD)
Z_STACK = {0: (0, 0), 1: (0, 1), 7: (0, 2), 2: (0, 3), 6: (1, 0), 3: (1, 1), 5: (1, 2), 4: (1, 3)}
Y_CODE = {0: 0, 3: 1, 1: 2, 2: 3}


def shift(v, axis, d, n):
    return lax.ppermute(v, axis, [(i, (i + d) % n) for i in range(n)])


zp = functools.partial(shift, axis="z", d=1, n=NZ)
zm = functools.partial(shift, axis="z", d=-1, n=NZ)
yp = functools.partial(shift, axis="y", d=1, n=NY)
ym = functools.partial(shift, axis="y", d=-1, n=NY)
xp = functools.partial(shift, axis="x", d=1, n=NX)
xm = functools.partial(shift, axis="x", d=-1, n=NX)
swap = functools.partial(shift, axis="c", d=1, n=NC)


def gate(vals, waits):
    return lax.optimization_barrier((vals, waits))


def gather_kv(kv, waits):
    zc, yc = kv[:ZROWS], kv[ZROWS:]
    hz, hy = ZROWS // 2, YROWS // 2
    y1p, y1m, z1p, z1m = yp(yc), ym(yc), zp(zc), zm(zc)
    (y1p, y1m, z1p, z1m), waits = gate((y1p, y1m, z1p, z1m), waits)
    y2p, y2m, z2p, z2m = yp(y1p[:hy]), ym(y1m[hy:]), zp(z1p), zm(z1m)
    s0 = jnp.stack([yc, y1p, y1m, jnp.concatenate([y2p, y2m])])
    a1p, a1m = zp(s0), zm(s0)
    z3p, z3m = zp(z2p), zm(z2m)
    g1 = jnp.stack([zc, z1m, z1p, z2m])
    g1p, g1m = yp(g1), ym(g1)
    (a1p, a1m), (z3p, z3m) = gate((a1p, a1m), (z3p, z3m))
    z4p, z4m = zp(z3p[:hz]), zm(z3m[hz:])
    a2p, a2m = zp(a1p), zm(a1m)
    g2 = jnp.stack([z2p, z3m, z3p, jnp.concatenate([z4p, z4m])])
    (g1p, g1m), g2 = gate((g1p, g1m), g2)
    g1x = yp(g1p)
    g2p, g2m = yp(g2), ym(g2)
    a3p, a3m = zp(a2p), zm(a2m)
    g2x = ym(g2m)
    a4p, a4m = zp(a3p[:2]), zm(a3m[2:])
    za = [g1, g1p, g1m, g1x, g2, g2p, g2m, g2x]
    ya = [s0, a1m, a2m, a3m, a4p, a3p, a2p, a1p, a4m]
    return za, ya, waits


def block_places(route, y, z):
    me = y * NZ + z
    dy, dz = (route // NZ - y) % NY, (route % NZ - z) % NZ
    pick = lambda table, i: jnp.asarray(table, jnp.int32)[i]
    ycode = pick([Y_CODE[i] for i in range(NY)], dy)
    group = pick([Z_STACK[i][0] for i in range(NZ)], dz)
    slot = pick([Z_STACK[i][1] for i in range(NZ)], dz)
    ok = (route < me).astype(jnp.int32)
    late = (dz == 4) & (ycode >= 2)
    yarray, yslot = jnp.where(late, NZ, dz), jnp.where(late, ycode - 2, ycode)
    return jnp.stack([group * 4 + ycode, slot, yarray, yslot, ok]).reshape(-1)


TILE = 128


def own_kernel(q_ref, kv_ref, m_ref, l_ref, o_ref):
    for h in range(HEADS):
        cols = slice(h * HD, (h + 1) * HD)
        for t in range(BLK // TILE):
            rows = slice(t * TILE, (t + 1) * TILE)
            n = (t + 1) * TILE
            s = lax.dot_general(
                q_ref[rows, cols], kv_ref[:n, :HD], (((1,), (1,)), ((), ())), preferred_element_type=jnp.float32
            )
            qpos = t * TILE + lax.broadcasted_iota(jnp.int32, (TILE, n), 0)
            s = jnp.where(qpos >= lax.broadcasted_iota(jnp.int32, (TILE, n), 1), s * SCALE, -1e30)
            m = jnp.max(s, axis=1, keepdims=True)
            e = jnp.exp2(s - m)
            m_ref[h, rows, :] = jnp.broadcast_to(m, (TILE, HD))
            l_ref[h, rows, :] = jnp.broadcast_to(jnp.sum(e, axis=1, keepdims=True), (TILE, HD))
            o_ref[rows, cols] = jnp.dot(e.astype(jnp.bfloat16), kv_ref[:n, HD:], preferred_element_type=jnp.float32)


def routed_kernel(place_ref, q_ref, m_ref, l_ref, o_ref, *rest):
    za, ya, out_ref, buf, sems = rest[:8], rest[8:17], rest[17], rest[18], rest[19]
    n = HEADS * SLOTS
    for u in range(n):
        for i, (arrays, first, size) in enumerate(((za, 0, ZROWS), (ya, ZROWS, YROWS))):
            for a, array in enumerate(arrays):

                @pl.when(place_ref[2 * i * n + u] == a)
                def _():
                    slot = place_ref[(2 * i + 1) * n + u]
                    pltpu.make_async_copy(array.at[slot], buf.at[u, pl.ds(first, size), pl.ds(0, 2 * HD)], sems.at[u, i]).start()

    for u in range(n):
        buf[u, :, 2 * HD :] = jnp.ones((BLK, HD), jnp.bfloat16)
    for h in range(HEADS):
        cols = slice(h * HD, (h + 1) * HD)
        for s in range(SLOTS):
            u = h * SLOTS + s
            pltpu.make_async_copy(za[0].at[0], buf.at[u, pl.ds(0, ZROWS), pl.ds(0, 2 * HD)], sems.at[u, 0]).wait()
            pltpu.make_async_copy(ya[0].at[0], buf.at[u, pl.ds(ZROWS, YROWS), pl.ds(0, 2 * HD)], sems.at[u, 1]).wait()
        for t in range(BLK // TILE):
            rows = slice(t * TILE, (t + 1) * TILE)
            scores = []
            m0 = m_ref[h, rows, :1]
            m = m0
            for s in range(SLOTS):
                u = h * SLOTS + s
                sc = lax.dot_general(
                    q_ref[rows, cols], buf[u, :, :HD], (((1,), (1,)), ((), ())), preferred_element_type=jnp.float32
                )
                top = jnp.max(sc, axis=1, keepdims=True) * SCALE
                m = jnp.maximum(m, jnp.where(place_ref[4 * n + u] == 1, top, -1e30))
                scores.append(sc)
            w0 = jnp.exp2(m0 - m)
            l = l_ref[h, rows, :] * w0
            acc = o_ref[rows, cols] * w0
            for s in range(SLOTS):
                u = h * SLOTS + s
                e = jnp.exp2(scores[s] * SCALE - jnp.where(place_ref[4 * n + u] == 1, m, 1e30)).astype(jnp.bfloat16)
                both = jnp.dot(e, buf[u, :, HD:], preferred_element_type=jnp.float32)
                acc = acc + both[:, :HD]
                l = l + both[:, HD:]
            out_ref[rows, cols] = (acc / l).astype(out_ref.dtype)


def near_kernel(at_ref, a0_ref, a1_ref, a2_ref, w_ref, out_ref, buf, sems):
    copies = [pltpu.make_async_copy(w_ref.at[at_ref[i]], buf.at[i], sems.at[i]) for i in range(3)]
    for copy in copies:
        copy.start()
    for i, a_ref in enumerate((a0_ref, a1_ref, a2_ref)):
        copies[i].wait()
        for n in range(NZ // 2):
            rows = jnp.concatenate([buf[i, 2 * n], buf[i, 2 * n + 1]], axis=1)
            part = jnp.dot(a_ref[...], rows, preferred_element_type=jnp.float32)
            cols = slice(n * 2 * HD, (n + 1) * 2 * HD)
            if i == 0:
                out_ref[:, cols] = part
            else:
                out_ref[:, cols] += part


def far_kernel(at_ref, total_ref, a0_ref, a1_ref, w_ref, out_ref, buf, sem):
    width = NZ * HD // NC
    copy = pltpu.make_async_copy(w_ref.at[at_ref[0], pl.ds(at_ref[1] * (NZ // NC), NZ // NC)], buf, sem)
    copy.start()
    copy.wait()
    for i, a_ref in enumerate((a0_ref, a1_ref)):
        rows = slice(i * (BLK // 2), (i + 1) * (BLK // 2))
        for n in range(NZ // NC // 2):
            part = jnp.dot(
                a_ref[...], jnp.concatenate([buf[2 * n], buf[2 * n + 1]], axis=1), preferred_element_type=jnp.float32
            )
            cols = pl.ds(pl.multiple_of(at_ref[1] * width, width) + n * 2 * HD, 2 * HD)
            out_ref[rows, n * 2 * HD : (n + 1) * 2 * HD] = (total_ref[rows, cols] + part).astype(out_ref.dtype)


def attention_own(q, kv):
    stat = jax.ShapeDtypeStruct((HEADS, BLK, HD), jnp.float32)
    return pl.pallas_call(
        own_kernel,
        out_shape=(stat, stat, jax.ShapeDtypeStruct((BLK, HEADS * HD), jnp.float32)),
        compiler_params=pltpu.CompilerParams(vmem_limit_bytes=32 << 20),
    )(q, kv)


def attention_routed(places, q, m, l, o, za, ya):
    n = HEADS * SLOTS
    vmem = pl.BlockSpec(memory_space=pltpu.VMEM)
    return pl.pallas_call(
        routed_kernel,
        out_shape=jax.ShapeDtypeStruct((BLK, HEADS * HD), jnp.bfloat16),
        in_specs=[pl.BlockSpec(memory_space=pltpu.SMEM)] + [vmem] * 4 + [pl.BlockSpec(memory_space=pl.ANY)] * 17,
        out_specs=vmem,
        scratch_shapes=[pltpu.VMEM((n, BLK, 3 * HD), jnp.bfloat16), pltpu.SemaphoreType.DMA((n, 2))],
        compiler_params=pltpu.CompilerParams(vmem_limit_bytes=32 << 20),
    )(places, q, m, l, o, *za, *ya)


def project_near(at, a0, a1, a2, w):
    vmem = pl.BlockSpec(memory_space=pltpu.VMEM)
    return pl.pallas_call(
        near_kernel,
        out_shape=jax.ShapeDtypeStruct((BLK, NZ * HD), jnp.float32),
        in_specs=[pl.BlockSpec(memory_space=pltpu.SMEM)] + [vmem] * 3 + [pl.BlockSpec(memory_space=pl.ANY)],
        out_specs=vmem,
        scratch_shapes=[pltpu.VMEM((3, NZ, BLK, HD), jnp.bfloat16), pltpu.SemaphoreType.DMA((3,))],
        compiler_params=pltpu.CompilerParams(vmem_limit_bytes=32 << 20),
    )(at, a0, a1, a2, w)


def project_far(at, total, a0, a1, w, dtype):
    vmem = pl.BlockSpec(memory_space=pltpu.VMEM)
    return pl.pallas_call(
        far_kernel,
        out_shape=jax.ShapeDtypeStruct((BLK, NZ * HD // NC), dtype),
        in_specs=[pl.BlockSpec(memory_space=pltpu.SMEM)] + [vmem] * 3 + [pl.BlockSpec(memory_space=pl.ANY)],
        out_specs=vmem,
        scratch_shapes=[pltpu.VMEM((NZ // NC, BLK, HD), jnp.bfloat16), pltpu.SemaphoreType.DMA],
        compiler_params=pltpu.CompilerParams(vmem_limit_bytes=32 << 20),
    )(at, total, a0, a1, w)


def body(queries, keys, values, routing, w_out):
    y, z, x, c = (lax.axis_index(a) for a in AXES)
    kv = jnp.concatenate([keys, values], axis=1)
    at = lambda y, z, x, c: ((y * NZ + z) * NX + x) * NC + c
    turn = [
        (at(y, z, x, c), at(x, z, y, c)) for y in range(NY) for z in range(NZ) for x in range(NX) for c in range(NC)
    ]
    w = lax.ppermute(w_out, AXES, turn)
    route = lax.dynamic_index_in_dim(routing, y * NZ + z, 0, keepdims=False)
    places = block_places(route.reshape(-1), y, z)
    m, l, o = attention_own(queries, kv)
    za, ya, (places, m, l, o, w) = gather_kv(kv, (places, m, l, o, w))
    w_all = lax.all_gather(lax.all_gather(w, "z", axis=0, tiled=False), "y", axis=0, tiled=False)
    attn = attention_routed(places, queries, m, l, o, za, ya)
    x1p, x1m = xp(attn), xm(attn)
    x2p, x2m = xp(x1p[: BLK // 2]), xm(x1m[BLK // 2 :])
    total = project_near(jnp.stack([x, (x - 1) % NX, (x + 1) % NX]), attn, x1p, x1m, w_all)
    far = (x + 2) % NX
    other = project_far(jnp.stack([far, 1 - c]), total, x2p, x2m, w_all, jnp.bfloat16)
    theirs = swap(other)
    mine = project_far(jnp.stack([far, c]), total, x2p, x2m, w_all, jnp.float32)
    return (mine + theirs.astype(jnp.float32)).astype(jnp.bfloat16)


def solution(mesh):
    grid = Mesh(mesh.devices.reshape(NY, NZ, NX, NC), AXES)
    seq, mp = ("y", "z"), ("x", "c")
    in_specs = (P(seq, mp), P(seq, mp), P(seq, mp), P(None, mp, None), P(mp, seq))
    return jax.shard_map(body, mesh=grid, in_specs=in_specs, out_specs=P(seq, mp), check_vma=False)
```

```python
import functools
import math

import jax
import jax.numpy as jnp
from jax import lax
from jax.experimental import pallas as pl
from jax.experimental.pallas import tpu as pltpu
from jax.sharding import Mesh, PartitionSpec as P

HD = 128
BLK = 512
HEADS = 4
SLOTS = 3
NY, NZ, NX, NC = 4, 8, 4, 2
AXES = ("y", "z", "x", "c")
HALF = BLK // 2
SCALE = math.log2(math.e) / math.sqrt(HD)
Z_STACK = {0: (0, 0), 1: (0, 1), 7: (0, 2), 2: (0, 3), 6: (1, 0), 3: (1, 1), 5: (1, 2), 4: (1, 3)}


def shift(v, axis, d, n):
    return lax.ppermute(v, axis, [(i, (i + d) % n) for i in range(n)])


zp = functools.partial(shift, axis="z", d=1, n=NZ)
zm = functools.partial(shift, axis="z", d=-1, n=NZ)
xp = functools.partial(shift, axis="x", d=1, n=NX)
xm = functools.partial(shift, axis="x", d=-1, n=NX)
swap = functools.partial(shift, axis="c", d=1, n=NC)


def gate(vals, waits):
    return lax.optimization_barrier((vals, waits))


def spread_y(v):
    return lax.all_to_all(jnp.broadcast_to(v[None], (NY,) + v.shape), "y", 0, 0, tiled=True)


def join(*parts):
    return jnp.concatenate(parts)


def gather(zc, yc, w, early):
    n = zc.shape[0]
    wa, wb = w[:HALF], w[HALF:]
    s0 = spread_y(yc)
    z1p, z1m = zp(zc), zm(zc)
    (z1p, z1m, wa, wb), early = gate((z1p, z1m, wa, wb), early)
    wb = spread_y(wb)
    z2p, z2m = zp(join(z1p, wa)), zm(join(z1m, wa))
    (z2p, z2m), s0 = gate((z2p, z2m), s0)
    a1p, a1m = zp(s0), zm(s0)
    z3p, z3m = zp(z2p), zm(z2m)
    g1 = spread_y(jnp.stack([zc, z1m, z1p, z2m[:n]]))
    (a1p, a1m), (z3p, z3m) = gate((a1p, a1m), (z3p, z3m))
    a2p, a2m = zp(a1p), zm(a1m)
    z4p, z4m = zp(join(z3p[: n // 2], z3p[n:])), zm(join(z3m[n // 2 : n], z3m[n:]))
    (a2p, a2m, wb), (z4p, z4m) = gate((a2p, a2m, wb), (z4p, z4m))
    a3p, a3m = zp(a2p), zm(a2m)
    g2 = spread_y(jnp.stack([z2p[:n], z3m[:n], z3p[:n], join(z4p[: n // 2], z4m[: n // 2])]))
    w3p, w3m = z4p[n // 2 :], z4m[n // 2 :]
    w4p, w4m = zp(w3p[: HALF // 2]), zm(w3m[HALF // 2 :])
    (a3p, a3m), (w4p, w4m) = gate((a3p, a3m), (w4p, w4m))
    a4p, a4m = zp(a3p[:2]), zm(a3m[2:])
    wa = [wa, z2m[n:], z2p[n:], z3m[n:], z3p[n:], w3m, w3p, join(w4p, w4m)]
    ((g1, g2, s0, a1p, a1m, a2p, a2m, a3p, a3m, a4p, a4m), (wa, wb)), _ = gate(
        ((g1, g2, s0, a1p, a1m, a2p, a2m, a3p, a3m, a4p, a4m), (wa, wb)), ()
    )
    return [g1, g2], [s0, a1m, a2m, a3m, a4p, a3p, a2p, a1p, a4m], jnp.stack(wa), wb, early


def block_places(route, y, z):
    me = y * NZ + z
    by, dz = route // NZ, (route % NZ - z) % NZ
    pick = lambda table: jnp.asarray(table, jnp.int32)[dz]
    late = (dz == 4) & (by >= 2)
    ok = (route < me).astype(jnp.int32)
    stack, slot = pick([Z_STACK[i][0] for i in range(NZ)]), pick([Z_STACK[i][1] for i in range(NZ)])
    return jnp.stack([stack, slot, jnp.where(late, NZ, dz), jnp.where(late, by - 2, by), ok, by]).reshape(-1)


TILE = 128


def own_kernel(q_ref, k_ref, v_ref, m_ref, l_ref, o_ref):
    for h in range(HEADS):
        cols = slice(h * HD, (h + 1) * HD)
        for t in range(BLK // TILE):
            rows = slice(t * TILE, (t + 1) * TILE)
            n = (t + 1) * TILE
            s = lax.dot_general(
                q_ref[rows, cols], k_ref[:n], (((1,), (1,)), ((), ())), preferred_element_type=jnp.float32
            )
            qpos = t * TILE + lax.broadcasted_iota(jnp.int32, (TILE, n), 0)
            s = jnp.where(qpos >= lax.broadcasted_iota(jnp.int32, (TILE, n), 1), s * SCALE, -1e30)
            m = jnp.max(s, axis=1, keepdims=True)
            e = jnp.exp2(s - m)
            m_ref[h, rows, :] = jnp.broadcast_to(m, (TILE, HD))
            l_ref[h, rows, :] = jnp.broadcast_to(jnp.sum(e, axis=1, keepdims=True), (TILE, HD))
            o_ref[rows, cols] = jnp.dot(e.astype(jnp.bfloat16), v_ref[:n], preferred_element_type=jnp.float32)


def routed_kernel(place_ref, q_ref, m_ref, l_ref, o_ref, *rest):
    za, ya, out_ref, kbuf, vbuf, sems = rest[:2], rest[2:11], rest[11], rest[12], rest[13], rest[14]
    n = HEADS * SLOTS

    def fetch(u, i, block):
        rows = pl.ds(i * HALF, HALF)
        pltpu.make_async_copy(block.at[pl.ds(0, HALF)], kbuf.at[u, rows], sems.at[u, i, 0]).start()
        pltpu.make_async_copy(block.at[pl.ds(HALF, HALF)], vbuf.at[u, rows, pl.ds(0, HD)], sems.at[u, i, 1]).start()

    for u in range(n):
        for a, array in enumerate(za):

            @pl.when(place_ref[u] == a)
            def _():
                fetch(u, 0, array.at[place_ref[5 * n + u], place_ref[n + u]])

        for a, array in enumerate(ya):

            @pl.when(place_ref[2 * n + u] == a)
            def _():
                fetch(u, 1, array.at[place_ref[3 * n + u]])

    for u in range(n):
        vbuf[u, :, HD:] = jnp.ones((BLK, HD), jnp.bfloat16)
    for h in range(HEADS):
        cols = slice(h * HD, (h + 1) * HD)
        for s in range(SLOTS):
            u = h * SLOTS + s
            for i in range(2):
                rows = pl.ds(i * HALF, HALF)
                some = ya[0].at[0, pl.ds(0, HALF)]
                pltpu.make_async_copy(some, kbuf.at[u, rows], sems.at[u, i, 0]).wait()
                pltpu.make_async_copy(some, vbuf.at[u, rows, pl.ds(0, HD)], sems.at[u, i, 1]).wait()
        for t in range(BLK // TILE):
            rows = slice(t * TILE, (t + 1) * TILE)
            scores = []
            m0 = m_ref[h, rows, :1]
            m = m0
            for s in range(SLOTS):
                u = h * SLOTS + s
                sc = lax.dot_general(
                    q_ref[rows, cols], kbuf[u], (((1,), (1,)), ((), ())), preferred_element_type=jnp.float32
                )
                top = jnp.max(sc, axis=1, keepdims=True) * SCALE
                m = jnp.maximum(m, jnp.where(place_ref[4 * n + u] == 1, top, -1e30))
                scores.append(sc)
            w0 = jnp.exp2(m0 - m)
            l = l_ref[h, rows, :] * w0
            acc = o_ref[rows, cols] * w0
            for s in range(SLOTS):
                u = h * SLOTS + s
                e = jnp.exp2(scores[s] * SCALE - jnp.where(place_ref[4 * n + u] == 1, m, 1e30)).astype(jnp.bfloat16)
                both = jnp.dot(e, vbuf[u], preferred_element_type=jnp.float32)
                acc = acc + both[:, :HD]
                l = l + both[:, HD:]
            out_ref[rows, cols] = (acc / l).astype(out_ref.dtype)


def fetch_rows(at_ref, x, first, count, wa_ref, wb_ref, buf, sem):
    for dz in range(NZ):
        col = lax.rem(at_ref[0] + dz, NZ) - first

        def start():
            a, s = Z_STACK[dz]
            pltpu.make_async_copy(wa_ref.at[x, a * 4 + s], buf.at[col, pl.ds(0, HALF)], sem).start()
            late = 1 if dz == 4 else 0
            b = wb_ref[dz].at[x] if not late else None
            if not late:
                pltpu.make_async_copy(b, buf.at[col, pl.ds(HALF, HALF)], sem).start()
            else:

                @pl.when(x < 2)
                def _():
                    pltpu.make_async_copy(wb_ref[4].at[x], buf.at[col, pl.ds(HALF, HALF)], sem).start()

                @pl.when(x >= 2)
                def _():
                    pltpu.make_async_copy(wb_ref[8].at[x - 2], buf.at[col, pl.ds(HALF, HALF)], sem).start()

        if count == NZ:
            start()
        else:
            pl.when((col >= 0) & (col < count))(start)
    return pltpu.make_async_copy(buf, buf, sem)


def near_kernel(at_ref, a0_ref, a1_ref, a2_ref, wa_ref, *rest):
    wb_ref, out_ref, buf, sems = rest[:9], rest[9], rest[10], rest[11]
    copies = [fetch_rows(at_ref, at_ref[1 + i], 0, NZ, wa_ref, wb_ref, buf.at[i], sems.at[i]) for i in range(3)]
    for i, a_ref in enumerate((a0_ref, a1_ref, a2_ref)):
        copies[i].wait()
        for n in range(NZ // 2):
            rows = jnp.concatenate([buf[i, 2 * n], buf[i, 2 * n + 1]], axis=1)
            part = jnp.dot(a_ref[...], rows, preferred_element_type=jnp.float32)
            cols = slice(n * 2 * HD, (n + 1) * 2 * HD)
            if i == 0:
                out_ref[:, cols] = part
            else:
                out_ref[:, cols] += part


def far_kernel(at_ref, total_ref, a0_ref, a1_ref, wa_ref, *rest):
    wb_ref, out_ref, buf, sem = rest[:9], rest[9], rest[10], rest[11]
    width, count = NZ * HD // NC, NZ // NC
    fetch_rows(at_ref, at_ref[1], at_ref[2] * count, count, wa_ref, wb_ref, buf, sem).wait()
    for i, a_ref in enumerate((a0_ref, a1_ref)):
        rows = slice(i * HALF, (i + 1) * HALF)
        for n in range(count // 2):
            part = jnp.dot(
                a_ref[...], jnp.concatenate([buf[2 * n], buf[2 * n + 1]], axis=1), preferred_element_type=jnp.float32
            )
            cols = pl.ds(pl.multiple_of(at_ref[2] * width, width) + n * 2 * HD, 2 * HD)
            out_ref[rows, n * 2 * HD : (n + 1) * 2 * HD] = (total_ref[rows, cols] + part).astype(out_ref.dtype)


def attention_own(q, k, v):
    stat = jax.ShapeDtypeStruct((HEADS, BLK, HD), jnp.float32)
    return pl.pallas_call(
        own_kernel,
        out_shape=(stat, stat, jax.ShapeDtypeStruct((BLK, HEADS * HD), jnp.float32)),
        compiler_params=pltpu.CompilerParams(vmem_limit_bytes=32 << 20),
    )(q, k, v)


def attention_routed(places, q, m, l, o, za, ya):
    n = HEADS * SLOTS
    vmem = pl.BlockSpec(memory_space=pltpu.VMEM)
    return pl.pallas_call(
        routed_kernel,
        out_shape=jax.ShapeDtypeStruct((BLK, HEADS * HD), jnp.bfloat16),
        in_specs=[pl.BlockSpec(memory_space=pltpu.SMEM)] + [vmem] * 4 + [pl.BlockSpec(memory_space=pl.ANY)] * 11,
        out_specs=vmem,
        scratch_shapes=[
            pltpu.VMEM((n, BLK, HD), jnp.bfloat16),
            pltpu.VMEM((n, BLK, 2 * HD), jnp.bfloat16),
            pltpu.SemaphoreType.DMA((n, 2, 2)),
        ],
        compiler_params=pltpu.CompilerParams(vmem_limit_bytes=32 << 20),
    )(places, q, m, l, o, *za, *ya)


def project_near(at, a0, a1, a2, wa, wb):
    vmem = pl.BlockSpec(memory_space=pltpu.VMEM)
    return pl.pallas_call(
        near_kernel,
        out_shape=jax.ShapeDtypeStruct((BLK, NZ * HD), jnp.float32),
        in_specs=[pl.BlockSpec(memory_space=pltpu.SMEM)] + [vmem] * 3 + [pl.BlockSpec(memory_space=pl.ANY)] * 10,
        out_specs=vmem,
        scratch_shapes=[pltpu.VMEM((3, NZ, BLK, HD), jnp.bfloat16), pltpu.SemaphoreType.DMA((3,))],
        compiler_params=pltpu.CompilerParams(vmem_limit_bytes=32 << 20),
    )(at, a0, a1, a2, wa, *wb)


def project_far(at, total, a0, a1, wa, wb, dtype):
    vmem = pl.BlockSpec(memory_space=pltpu.VMEM)
    return pl.pallas_call(
        far_kernel,
        out_shape=jax.ShapeDtypeStruct((BLK, NZ * HD // NC), dtype),
        in_specs=[pl.BlockSpec(memory_space=pltpu.SMEM)] + [vmem] * 3 + [pl.BlockSpec(memory_space=pl.ANY)] * 10,
        out_specs=vmem,
        scratch_shapes=[pltpu.VMEM((NZ // NC, BLK, HD), jnp.bfloat16), pltpu.SemaphoreType.DMA],
        compiler_params=pltpu.CompilerParams(vmem_limit_bytes=32 << 20),
    )(at, total, a0, a1, wa, *wb)


def body(queries, keys, values, routing, w_out):
    y, z, x, c = (lax.axis_index(a) for a in AXES)
    at = lambda y, z, x, c: ((y * NZ + z) * NX + x) * NC + c
    turn = [
        (at(y, z, x, c), at(x, z, y, c)) for y in range(NY) for z in range(NZ) for x in range(NX) for c in range(NC)
    ]
    w = lax.ppermute(w_out, AXES, turn)
    route = lax.dynamic_index_in_dim(routing, y * NZ + z, 0, keepdims=False)
    places = block_places(route.reshape(-1), y, z)
    m, l, o = attention_own(queries, keys, values)
    zc, yc = join(keys[:HALF], values[:HALF]), join(keys[HALF:], values[HALF:])
    za, ya, wa, wb, (places, m, l, o) = gather(zc, yc, w, (places, m, l, o))
    wa = spread_y(wa)
    w1p, w1m = zp(wb), zm(wb)
    attn = attention_routed(places, queries, m, l, o, za, ya)
    x1p, x1m = xp(attn), xm(attn)
    w2p, w2m = zp(w1p), zm(w1m)
    (x1p, x1m), (w2p, w2m) = gate((x1p, x1m), (w2p, w2m))
    x2p, x2m = xp(x1p[:HALF]), xm(x1m[HALF:])
    w3p, w3m = zp(w2p), zm(w2m)
    w4p, w4m = zp(w3p[:2]), zm(w3m[2:])
    wb = [wb, w1m, w2m, w3m, w4p, w3p, w2p, w1p, w4m]
    total = project_near(jnp.stack([z, x, (x - 1) % NX, (x + 1) % NX]), attn, x1p, x1m, wa, wb)
    far = (x + 2) % NX
    other = project_far(jnp.stack([z, far, 1 - c]), total, x2p, x2m, wa, wb, jnp.bfloat16)
    theirs = swap(other)
    mine = project_far(jnp.stack([z, far, c]), total, x2p, x2m, wa, wb, jnp.float32)
    return (mine + theirs.astype(jnp.float32)).astype(jnp.bfloat16)


def solution(mesh):
    grid = Mesh(mesh.devices.reshape(NY, NZ, NX, NC), AXES)
    seq, mp = ("y", "z"), ("x", "c")
    in_specs = (P(seq, mp), P(seq, mp), P(seq, mp), P(None, mp, None), P(mp, seq))
    return jax.shard_map(body, mesh=grid, in_specs=in_specs, out_specs=P(seq, mp), check_vma=False)
```

```python
import functools
import math

import jax
import jax.numpy as jnp
from jax import lax
from jax.experimental import pallas as pl
from jax.experimental.pallas import tpu as pltpu
from jax.sharding import Mesh, PartitionSpec as P

HD = 128
BLK = 512
HEADS = 4
SLOTS = 3
NY, NZ, NX, NC = 4, 8, 4, 2
AXES = ("y", "z", "x", "c")
HALF = BLK // 2
SCALE = math.log2(math.e) / math.sqrt(HD)
def shift(v, axis, d, n):
    return lax.ppermute(v, axis, [(i, (i + d) % n) for i in range(n)])


zp = functools.partial(shift, axis="z", d=1, n=NZ)
zm = functools.partial(shift, axis="z", d=-1, n=NZ)
yp = functools.partial(shift, axis="y", d=1, n=NY)
ym = functools.partial(shift, axis="y", d=-1, n=NY)
xp = functools.partial(shift, axis="x", d=1, n=NX)
xm = functools.partial(shift, axis="x", d=-1, n=NX)
swap = functools.partial(shift, axis="c", d=1, n=NC)


def gate(vals, waits):
    return lax.optimization_barrier((vals, waits))


def join(*parts):
    return jnp.concatenate(parts)


def gather(zc, yc, w, early):
    n = zc.shape[0]
    y1p, y1m, z1p, z1m = yp(yc), ym(yc), zp(zc), zm(zc)
    (y1p, y1m, z1p, z1m), w = gate((y1p, y1m, z1p, z1m), w)
    w = lax.all_gather(w, "z", axis=0, tiled=False)
    y2p, y2m, z2p, z2m = yp(y1p[: n // 2]), ym(y1m[n // 2 :]), zp(z1p), zm(z1m)
    (y2p, y2m, z2p, z2m), early = gate((y2p, y2m, z2p, z2m), early)
    s0 = jnp.stack([yc, y1p, y1m, join(y2p, y2m)])
    g1 = jnp.stack([zc, z1m, z1p, z2m])
    a1p, a1m, g1p, g1m, z3p = zp(s0), zm(s0), yp(g1), ym(g1), zp(z2p)
    (a1p, a1m, g1p, g1m, z3p, z2m), _ = gate((a1p, a1m, g1p, g1m, z3p, z2m), ())
    a2p, a2m, z4p, z3m, g1x = zp(a1p), zm(a1m), zp(z3p), zm(z2m), yp(g1p)
    (a2p, a2m, z4p, z3m, g1x), w = gate((a2p, a2m, z4p, z3m, g1x), w)
    w = lax.all_gather(w, "y", axis=0, tiled=False)
    g2 = jnp.stack([z2p, z3m, z3p, z4p])
    a3p, a3m, g2p, g2m = zp(a2p), zm(a2m), yp(g2), ym(g2)
    (a3p, a3m, g2p, g2m), _ = gate((a3p, a3m, g2p, g2m), ())
    a4p, a4m, g2h, g2l = zp(a3p[:2]), zm(a3m[2:]), yp(g2p[:2]), ym(g2m[2:])
    za = [g1, g1p, g1m, g1x, g2, g2p, g2m, g2h, g2l]
    ya = [s0, a1m, a2m, a3m, a4p, a3p, a2p, a1p, a4m]
    return za, ya, w, early


def block_places(route, y, z):
    by, dz = route // NZ, (route - z) % NZ
    dy = (by - y) % NY
    first = (dz == 0) | (dz == 1) | (dz == 7) | (dz == 2)
    zslot = jnp.where((dz == 1) | (dz == 3), 1, jnp.where((dz == 7) | (dz == 5), 2, jnp.where((dz == 2) | (dz == 4), 3, 0)))
    yslot = jnp.where(dy == 0, 0, jnp.where(dy == 3, 1, jnp.where(dy == 1, 2, 3)))
    zarray = jnp.where(first, 0, 4) + yslot
    tail = (zarray == 7) & (zslot >= 2)
    late = (dz == 4) & (yslot >= 2)
    zarray, zslot = jnp.where(tail, 8, zarray), jnp.where(tail, zslot - 2, zslot)
    yarray, yslot = jnp.where(late, NZ, dz), jnp.where(late, yslot - 2, yslot)
    ok = (route < y * NZ + z).astype(jnp.int32)
    return jnp.stack([zarray, zslot, yarray, yslot, ok]).reshape(-1)


TILE = 128


def attend_kernel(place_ref, q_ref, k_ref, v_ref, *rest):
    za, ya, out_ref, kbuf, vbuf, sems = rest[:9], rest[9:18], rest[18], rest[19], rest[20], rest[21]
    n = HEADS * SLOTS

    def fetch(u, i, block):
        rows = pl.ds(i * HALF, HALF)
        pltpu.make_async_copy(block.at[pl.ds(0, HALF)], kbuf.at[u, rows], sems.at[u, i, 0]).start()
        pltpu.make_async_copy(block.at[pl.ds(HALF, HALF)], vbuf.at[u, rows, pl.ds(0, HD)], sems.at[u, i, 1]).start()

    def choose(u, i, arrays):
        array, slot = place_ref[2 * i * n + u], place_ref[(2 * i + 1) * n + u]
        for low, high in ((0, 4), (4, 9)):

            @pl.when((array >= low) & (array < high))
            def _():
                for a in range(low, high):

                    @pl.when(array == a)
                    def _():
                        fetch(u, i, arrays[a].at[slot])

    for u in range(n):
        choose(u, 0, za)
        choose(u, 1, ya)
    for u in range(n + 1):
        vbuf[u, :, HD:] = jnp.ones((BLK, HD), jnp.bfloat16)
    vbuf[n, :, :HD] = v_ref[...]
    scores_of = lambda q, k: lax.dot_general(q, k, (((1,), (1,)), ((), ())), preferred_element_type=jnp.float32)
    for h in range(HEADS):
        cols = slice(h * HD, (h + 1) * HD)
        for s in range(SLOTS):
            u = h * SLOTS + s
            for i in range(2):
                rows = pl.ds(i * HALF, HALF)
                some = za[0].at[0, pl.ds(0, HALF)]
                pltpu.make_async_copy(some, kbuf.at[u, rows], sems.at[u, i, 0]).wait()
                pltpu.make_async_copy(some, vbuf.at[u, rows, pl.ds(0, HD)], sems.at[u, i, 1]).wait()
        for t in range(BLK // TILE):
            rows = slice(t * TILE, (t + 1) * TILE)
            q = q_ref[rows, cols]
            seen = (t + 1) * TILE
            own = scores_of(q, k_ref[:seen])
            later = lax.broadcasted_iota(jnp.int32, (TILE, seen), 1) - t * TILE
            own = jnp.where(lax.broadcasted_iota(jnp.int32, (TILE, seen), 0) >= later, own, -1e30)
            m = jnp.max(own, axis=1, keepdims=True) * SCALE
            scores = []
            for s in range(SLOTS):
                u = h * SLOTS + s
                sc = scores_of(q, kbuf[u])
                top = jnp.max(sc, axis=1, keepdims=True) * SCALE
                m = jnp.maximum(m, jnp.where(place_ref[4 * n + u] == 1, top, -1e30))
                scores.append(sc)
            e = jnp.exp2(own * SCALE - m).astype(jnp.bfloat16)
            both = jnp.dot(e, vbuf[n, :seen], preferred_element_type=jnp.float32)
            for s in range(SLOTS):
                u = h * SLOTS + s
                e = jnp.exp2(scores[s] * SCALE - jnp.where(place_ref[4 * n + u] == 1, m, 1e30)).astype(jnp.bfloat16)
                both = both + jnp.dot(e, vbuf[u], preferred_element_type=jnp.float32)
            out_ref[rows, cols] = (both[:, :HD] / both[:, HD:]).astype(out_ref.dtype)


def near_kernel(at_ref, a0_ref, a1_ref, a2_ref, w_ref, out_ref, buf, sems):
    copies = [pltpu.make_async_copy(w_ref.at[at_ref[i]], buf.at[i], sems.at[i]) for i in range(3)]
    for copy in copies:
        copy.start()
    for copy in copies:
        copy.wait()
    for n in range(NZ // 2):
        total = None
        for i, a_ref in enumerate((a0_ref, a1_ref, a2_ref)):
            rows = jnp.concatenate([buf[i, 2 * n], buf[i, 2 * n + 1]], axis=1)
            part = jnp.dot(a_ref[...], rows, preferred_element_type=jnp.float32)
            total = part if total is None else total + part
        out_ref[:, n * 2 * HD : (n + 1) * 2 * HD] = total


def far_kernel(at_ref, total_ref, a0_ref, a1_ref, w_ref, out_ref, buf, sem):
    width, count = NZ * HD // NC, NZ // NC
    copy = pltpu.make_async_copy(w_ref.at[at_ref[0], pl.ds(at_ref[1] * count, count)], buf, sem)
    copy.start()
    copy.wait()
    for i, a_ref in enumerate((a0_ref, a1_ref)):
        rows = slice(i * HALF, (i + 1) * HALF)
        for n in range(count // 2):
            part = jnp.dot(
                a_ref[...], jnp.concatenate([buf[2 * n], buf[2 * n + 1]], axis=1), preferred_element_type=jnp.float32
            )
            cols = pl.ds(pl.multiple_of(at_ref[1] * width, width) + n * 2 * HD, 2 * HD)
            out_ref[rows, n * 2 * HD : (n + 1) * 2 * HD] = (total_ref[rows, cols] + part).astype(out_ref.dtype)


def call(kernel, out_shape, scalars, near, far, scratch, flops, exps=0, vmem=32):
    spec = lambda space, arrays: [pl.BlockSpec(memory_space=space)] * len(arrays)
    return pl.pallas_call(
        kernel,
        out_shape=out_shape,
        in_specs=spec(pltpu.SMEM, scalars) + spec(pltpu.VMEM, near) + spec(pl.ANY, far),
        out_specs=jax.tree.map(lambda _: pl.BlockSpec(memory_space=pltpu.VMEM), out_shape),
        scratch_shapes=scratch,
        compiler_params=pltpu.CompilerParams(vmem_limit_bytes=vmem << 20),
        cost_estimate=pl.CostEstimate(flops=flops, transcendentals=exps, bytes_accessed=8 << 20),
    )(*scalars, *near, *far)


def attention(places, q, k, v, za, ya):
    n = HEADS * SLOTS
    scratch = [
        pltpu.VMEM((n, BLK, HD), jnp.bfloat16),
        pltpu.VMEM((n + 1, BLK, 2 * HD), jnp.bfloat16),
        pltpu.SemaphoreType.DMA((n, 2, 2)),
    ]
    out = jax.ShapeDtypeStruct((BLK, HEADS * HD), jnp.bfloat16)
    flops, exps = 6 * (n + HEADS) * BLK * BLK * HD, (n + HEADS) * BLK * BLK
    return call(attend_kernel, out, (places,), (q, k, v), (*za, *ya), scratch, flops, exps, 56)


def project_near(at, a0, a1, a2, w):
    out = jax.ShapeDtypeStruct((BLK, NZ * HD), jnp.float32)
    scratch = [pltpu.VMEM((3, NZ, BLK, HD), jnp.bfloat16), pltpu.SemaphoreType.DMA((3,))]
    return call(near_kernel, out, (at,), (a0, a1, a2), (w,), scratch, 6 * BLK * BLK * NZ * HD)


def project_far(at, total, a0, a1, w, dtype):
    out = jax.ShapeDtypeStruct((BLK, NZ * HD // NC), dtype)
    scratch = [pltpu.VMEM((NZ // NC, BLK, HD), jnp.bfloat16), pltpu.SemaphoreType.DMA]
    return call(far_kernel, out, (at,), (total, a0, a1), (w,), scratch, 2 * BLK * BLK * NZ * HD // NC)


def body(queries, keys, values, routing, w_out):
    y, z, x, c = (lax.axis_index(a) for a in AXES)
    at = lambda y, z, x, c: ((y * NZ + z) * NX + x) * NC + c
    turn = [
        (at(y, z, x, c), at(x, z, y, c)) for y in range(NY) for z in range(NZ) for x in range(NX) for c in range(NC)
    ]
    w = lax.ppermute(w_out, AXES, turn)
    route = lax.dynamic_index_in_dim(routing, y * NZ + z, 0, keepdims=False)
    places = block_places(route.reshape(-1), y, z)
    zc, yc = join(keys[:HALF], values[:HALF]), join(keys[HALF:], values[HALF:])
    za, ya, w, places = gather(zc, yc, w, places)
    attn = attention(places, queries, keys, values, za, ya)
    x1p, x1m = xp(attn), xm(attn)
    x2p, x2m = xp(x1p[:HALF]), xm(x1m[HALF:])
    total = project_near(jnp.stack([x, (x - 1) % NX, (x + 1) % NX]), attn, x1p, x1m, w)
    far = (x + 2) % NX
    other = project_far(jnp.stack([far, 1 - c]), total, x2p, x2m, w, jnp.bfloat16)
    theirs = swap(other)
    mine = project_far(jnp.stack([far, c]), total, x2p, x2m, w, jnp.float32)
    return (mine + theirs.astype(jnp.float32)).astype(jnp.bfloat16)


def solution(mesh):
    grid = Mesh(mesh.devices.reshape(NY, NZ, NX, NC), AXES)
    seq, mp = ("y", "z"), ("x", "c")
    in_specs = (P(seq, mp), P(seq, mp), P(seq, mp), P(None, mp, None), P(mp, seq))
    return jax.shard_map(body, mesh=grid, in_specs=in_specs, out_specs=P(seq, mp), check_vma=False)
```

```python
import functools
import math

import jax
import jax.numpy as jnp
from jax import lax
from jax.experimental import pallas as pl
from jax.experimental.pallas import tpu as pltpu
from jax.sharding import Mesh, PartitionSpec as P

HD = 128
BLK = 512
HEADS = 4
SLOTS = 3
NY, NZ, NX, NC = 4, 8, 4, 2
AXES = ("y", "z", "x", "c")
HALF = BLK // 2
SCALE = math.log2(math.e) / math.sqrt(HD)
def shift(v, axis, d, n):
    return lax.ppermute(v, axis, [(i, (i + d) % n) for i in range(n)])


zp = functools.partial(shift, axis="z", d=1, n=NZ)
zm = functools.partial(shift, axis="z", d=-1, n=NZ)
yp = functools.partial(shift, axis="y", d=1, n=NY)
ym = functools.partial(shift, axis="y", d=-1, n=NY)
y2 = functools.partial(shift, axis="y", d=2, n=NY)
xp = functools.partial(shift, axis="x", d=1, n=NX)
xm = functools.partial(shift, axis="x", d=-1, n=NX)
swap = functools.partial(shift, axis="c", d=1, n=NC)


def gate(vals, waits):
    return lax.optimization_barrier((vals, waits))


def join(*parts):
    return jnp.concatenate(parts)


def gather(zc, yc, w, turn, early):
    n = yc.shape[0] // 2
    y1p, y1m, z1p, z1m = yp(yc), ym(yc), zp(zc), zm(zc)
    w = lax.ppermute(w, AXES, turn)
    (y1p, y1m, z1p, z1m, w), _ = gate((y1p, y1m, z1p, z1m, w), ())
    both_p, both_m, w2, z2p, z2m = yp(join(y1p[:n], w)), ym(join(y1m[n:], w)), y2(w), zp(z1p), zm(z1m)
    (both_p, both_m, w2, z2p, z2m), early = gate((both_p, both_m, w2, z2p, z2m), early)
    y2p, y2m, w = both_p[:n], both_m[:n], jnp.stack([w, both_p[n:], both_m[n:], w2])
    s0 = jnp.concatenate([jnp.stack([yc, y1p, y1m, join(y2p, y2m)]), w], axis=1)
    g1 = jnp.stack([zc, z1m, z1p, z2m])
    s1p, s1m, g1p, g1m, z3p = zp(s0), zm(s0), yp(g1), ym(g1), zp(z2p)
    (s1p, s1m, g1p, g1m, z3p, z2m), _ = gate((s1p, s1m, g1p, g1m, z3p, z2m), ())
    s2p, s2m, z4p, z3m, g1x = zp(s1p), zm(s1m), zp(z3p), zm(z2m), yp(g1p)
    (s2p, s2m, z4p, z3m, g1x), _ = gate((s2p, s2m, z4p, z3m, g1x), ())
    g2 = jnp.stack([z2p, z3m, z3p, z4p])
    s3p, s3m, g2p, g2m = zp(s2p), zm(s2m), yp(g2), ym(g2)
    (s3p, s3m, g2p, g2m), _ = gate((s3p, s3m, g2p, g2m), ())
    s4p, s4m, g2h, g2l = zp(s3p[:2]), zm(s3m[2:]), yp(g2p[:2]), ym(g2m[2:])
    za = [g1, g1p, g1m, g1x, g2, g2p, g2m, g2h, g2l]
    ya = [s0, s1m, s2m, s3m, s4p, s3p, s2p, s1p, s4m]
    return za, ya, early


def block_places(route, y, z):
    by, dz = route // NZ, (route - z) % NZ
    dy = (by - y) % NY
    first = (dz == 0) | (dz == 1) | (dz == 7) | (dz == 2)
    zslot = jnp.where((dz == 1) | (dz == 3), 1, jnp.where((dz == 7) | (dz == 5), 2, jnp.where((dz == 2) | (dz == 4), 3, 0)))
    yslot = jnp.where(dy == 0, 0, jnp.where(dy == 3, 1, jnp.where(dy == 1, 2, 3)))
    zarray = jnp.where(first, 0, 4) + yslot
    tail = (zarray == 7) & (zslot >= 2)
    late = (dz == 4) & (yslot >= 2)
    zarray, zslot = jnp.where(tail, 8, zarray), jnp.where(tail, zslot - 2, zslot)
    yarray, yslot = jnp.where(late, NZ, dz), jnp.where(late, yslot - 2, yslot)
    ok = (route < y * NZ + z).astype(jnp.int32)
    return jnp.stack([zarray, zslot, yarray, yslot, ok]).reshape(-1)


TILE = 128


def attend_kernel(place_ref, q_ref, k_ref, v_ref, *rest):
    za, ya, out_ref, kbuf, vbuf, sems = rest[:9], rest[9:18], rest[18], rest[19], rest[20], rest[21]
    n = HEADS * SLOTS

    def copies(u, i, block):
        half = lambda first, at: pltpu.make_async_copy(
            block.at[pl.ds(first, HALF)], vbuf.at[u, pl.ds(at, HALF), pl.ds(0, HD)], sems.at[u, i, 1]
        )
        if i == 1:
            return [half(0, HALF)]
        return [pltpu.make_async_copy(block.at[pl.ds(0, BLK)], kbuf.at[u], sems.at[u, i, 0]), half(BLK, 0)]

    for u in range(n):
        for i, arrays in enumerate((za, ya)):
            array, slot = place_ref[2 * i * n + u], place_ref[(2 * i + 1) * n + u]
            for low, high in ((0, 4), (4, 9)):

                @pl.when((array >= low) & (array < high))
                def _():
                    for a in range(low, high):

                        @pl.when(array == a)
                        def _():
                            for copy in copies(u, i, arrays[a].at[slot]):
                                copy.start()

    for u in range(n + 1):
        vbuf[u, :, HD:] = jnp.ones((BLK, HD), jnp.bfloat16)
    vbuf[n, :, :HD] = v_ref[...]
    scores_of = lambda q, k: lax.dot_general(q, k, (((1,), (1,)), ((), ())), preferred_element_type=jnp.float32)
    for h in range(HEADS):
        cols = slice(h * HD, (h + 1) * HD)
        for s in range(SLOTS):
            u = h * SLOTS + s
            for i, arrays in enumerate((za, ya)):
                for copy in copies(u, i, arrays[0].at[0]):
                    copy.wait()
        for t in range(BLK // TILE):
            rows = slice(t * TILE, (t + 1) * TILE)
            q = q_ref[rows, cols]
            seen = (t + 1) * TILE
            own = scores_of(q, k_ref[:seen])
            later = lax.broadcasted_iota(jnp.int32, (TILE, seen), 1) - t * TILE
            own = jnp.where(lax.broadcasted_iota(jnp.int32, (TILE, seen), 0) >= later, own, -1e30)
            m = jnp.max(own, axis=1, keepdims=True) * SCALE
            scores = []
            for s in range(SLOTS):
                u = h * SLOTS + s
                sc = scores_of(q, kbuf[u])
                top = jnp.max(sc, axis=1, keepdims=True) * SCALE
                m = jnp.maximum(m, jnp.where(place_ref[4 * n + u] == 1, top, -1e30))
                scores.append(sc)
            e = jnp.exp2(own * SCALE - m).astype(jnp.bfloat16)
            both = jnp.dot(e, vbuf[n, :seen], preferred_element_type=jnp.float32)
            for s in range(SLOTS):
                u = h * SLOTS + s
                e = jnp.exp2(scores[s] * SCALE - jnp.where(place_ref[4 * n + u] == 1, m, 1e30)).astype(jnp.bfloat16)
                both = both + jnp.dot(e, vbuf[u], preferred_element_type=jnp.float32)
            out_ref[rows, cols] = (both[:, :HD] / both[:, HD:]).astype(out_ref.dtype)


def own_kernel(at_ref, a_ref, *rest):
    arrays, total_ref, near_ref, far_ref, buf, sems = rest[:9], rest[9], rest[10], rest[11], rest[12], rest[13]
    dests = (buf, near_ref.at[0], near_ref.at[1], far_ref)
    for i, dest in enumerate(dests):
        slot = at_ref[1 + i]
        for dz in range(NZ):
            col = (at_ref[0] + dz) & (NZ - 1)

            def copy(array, at):
                pltpu.make_async_copy(array.at[at, pl.ds(HALF, BLK)], dest.at[col], sems.at[i]).start()

            if dz == 4:
                pl.when(slot < 2)(lambda: copy(arrays[4], slot))
                pl.when(slot >= 2)(lambda: copy(arrays[8], slot - 2))
            else:
                copy(arrays[dz], slot)
    pltpu.make_async_copy(buf, buf, sems.at[0]).wait()
    for n in range(NZ // 2):
        cols = jnp.concatenate([buf[2 * n], buf[2 * n + 1]], axis=1)
        total_ref[:, n * 2 * HD : (n + 1) * 2 * HD] = jnp.dot(a_ref[...], cols, preferred_element_type=jnp.float32)
    for i, dest in enumerate(dests[1:]):
        pltpu.make_async_copy(dest, dest, sems.at[1 + i]).wait()


def near_kernel(total_ref, a0_ref, a1_ref, w_ref, out_ref):
    for n in range(NZ // 2):
        cols = slice(n * 2 * HD, (n + 1) * 2 * HD)
        total = total_ref[:, cols]
        for i, a_ref in enumerate((a0_ref, a1_ref)):
            rows = jnp.concatenate([w_ref[i, 2 * n], w_ref[i, 2 * n + 1]], axis=1)
            total = total + jnp.dot(a_ref[...], rows, preferred_element_type=jnp.float32)
        out_ref[:, cols] = total


def far_kernel(core_ref, total_ref, a0_ref, a1_ref, w_ref, out_ref):
    width, count = NZ * HD // NC, NZ // NC
    core = core_ref[0]
    for i, a_ref in enumerate((a0_ref, a1_ref)):
        rows = slice(i * HALF, (i + 1) * HALF)
        for n in range(count // 2):
            right = jnp.concatenate([w_ref[core * count + 2 * n], w_ref[core * count + 2 * n + 1]], axis=1)
            part = jnp.dot(a_ref[...], right, preferred_element_type=jnp.float32)
            cols = pl.ds(pl.multiple_of(core * width, width) + n * 2 * HD, 2 * HD)
            out_ref[rows, n * 2 * HD : (n + 1) * 2 * HD] = (total_ref[rows, cols] + part).astype(out_ref.dtype)


def call(kernel, out_shape, scalars, near, far, scratch, flops, exps=0, vmem=32):
    spec = lambda space, arrays: [pl.BlockSpec(memory_space=space)] * len(arrays)
    return pl.pallas_call(
        kernel,
        out_shape=out_shape,
        in_specs=spec(pltpu.SMEM, scalars) + spec(pltpu.VMEM, near) + spec(pl.ANY, far),
        out_specs=jax.tree.map(lambda _: pl.BlockSpec(memory_space=pltpu.VMEM), out_shape),
        scratch_shapes=scratch,
        compiler_params=pltpu.CompilerParams(vmem_limit_bytes=vmem << 20),
        cost_estimate=pl.CostEstimate(flops=flops, transcendentals=exps, bytes_accessed=8 << 20),
    )(*scalars, *near, *far)


def attention(places, q, k, v, za, ya):
    n = HEADS * SLOTS
    scratch = [
        pltpu.VMEM((n, BLK, HD), jnp.bfloat16),
        pltpu.VMEM((n + 1, BLK, 2 * HD), jnp.bfloat16),
        pltpu.SemaphoreType.DMA((n, 2, 2)),
    ]
    out = jax.ShapeDtypeStruct((BLK, HEADS * HD), jnp.bfloat16)
    flops, exps = 6 * (n + HEADS) * BLK * BLK * HD, (n + HEADS) * BLK * BLK
    return call(attend_kernel, out, (places,), (q, k, v), (*za, *ya), scratch, flops, exps, 56)


def project_own(at, a, w):
    total = jax.ShapeDtypeStruct((BLK, NZ * HD), jnp.float32)
    rows = lambda *n: jax.ShapeDtypeStruct((*n, NZ, BLK, HD), jnp.bfloat16)
    scratch = [pltpu.VMEM((NZ, BLK, HD), jnp.bfloat16), pltpu.SemaphoreType.DMA((4,))]
    return call(own_kernel, (total, rows(2), rows()), (at,), (a,), w, scratch, 2 * BLK * BLK * NZ * HD, vmem=56)


def project_near(total, a0, a1, w):
    out = jax.ShapeDtypeStruct((BLK, NZ * HD), jnp.float32)
    return call(near_kernel, out, (), (total, a0, a1, w), (), (), 4 * BLK * BLK * NZ * HD)


def project_far(core, total, a0, a1, w, dtype):
    out = jax.ShapeDtypeStruct((BLK, NZ * HD // NC), dtype)
    return call(far_kernel, out, (core[None],), (total, a0, a1, w), (), (), 2 * BLK * BLK * NZ * HD // NC)


def body(queries, keys, values, routing, w_out):
    y, z, x, c = (lax.axis_index(a) for a in AXES)
    at = lambda y, z, x, c: ((y * NZ + z) * NX + x) * NC + c
    turn = [
        (at(y, z, x, c), at(x, z, y, c)) for y in range(NY) for z in range(NZ) for x in range(NX) for c in range(NC)
    ]
    route = lax.dynamic_index_in_dim(routing, y * NZ + z, 0, keepdims=False)
    places = block_places(route.reshape(-1), y, z)
    zc, yc = join(keys, values[:HALF]), values[HALF:]
    rows_of = lambda x: jnp.asarray([0, 2, 3, 1], jnp.int32)[(x - y) % NX]
    at = jnp.stack([z] + [rows_of(x + d) for d in (0, -1, 1, 2)])
    za, ya, (places, at) = gather(zc, yc, w_out, turn, (places, at))
    attn = attention(places, queries, keys, values, za, ya)
    x1p, x1m = xp(attn), xm(attn)
    (x1p, x1m), (total, near, far) = gate((x1p, x1m), project_own(at, attn, ya))
    x2p, x2m = xp(x1p[:HALF]), xm(x1m[HALF:])
    total = project_near(total, x1p, x1m, near)
    theirs = swap(project_far(1 - c, total, x2p, x2m, far, jnp.bfloat16))
    mine = project_far(c, total, x2p, x2m, far, jnp.float32)
    return (mine + theirs.astype(jnp.float32)).astype(jnp.bfloat16)


def solution(mesh):
    grid = Mesh(mesh.devices.reshape(NY, NZ, NX, NC), AXES)
    seq, mp = ("y", "z"), ("x", "c")
    in_specs = (P(seq, mp), P(seq, mp), P(seq, mp), P(None, mp, None), P(mp, seq))
    return jax.shard_map(body, mesh=grid, in_specs=in_specs, out_specs=P(seq, mp), check_vma=False)
```

```python
import functools
import math

import jax
import jax.numpy as jnp
from jax import lax
from jax.experimental import pallas as pl
from jax.experimental.pallas import tpu as pltpu
from jax.sharding import Mesh, PartitionSpec as P

HD = 128
BLK = 512
HEADS = 4
SLOTS = 3
NY, NZ, NX, NC = 4, 8, 4, 2
AXES = ("y", "z", "x", "c")
ARRAYS = ("kv", "z1m", "z1p", "z2m", "z2p", "s1m", "s1p", "s2p", "g0p", "g0m")
ARRAYS += ("gap", "gam", "gbp", "gbm", "gcp", "gcm", "gdp")
HALF = BLK // 2
ZROWS = 896
ZVALUES = ZROWS - BLK
LAST = BLK - ZVALUES
SLOT = LAST + BLK
SCALE = math.log2(math.e) / math.sqrt(HD)
def shift(v, axis, d, n):
    return lax.ppermute(v, axis, [(i, (i + d) % n) for i in range(n)])


zp = functools.partial(shift, axis="z", d=1, n=NZ)
zm = functools.partial(shift, axis="z", d=-1, n=NZ)
yp = functools.partial(shift, axis="y", d=1, n=NY)
ym = functools.partial(shift, axis="y", d=-1, n=NY)
y2 = functools.partial(shift, axis="y", d=2, n=NY)
xp = functools.partial(shift, axis="x", d=1, n=NX)
xm = functools.partial(shift, axis="x", d=-1, n=NX)
swap = functools.partial(shift, axis="c", d=1, n=NC)


def gate(vals, waits):
    return lax.optimization_barrier((vals, waits))


def join(*parts):
    return jnp.concatenate(parts)


def places():
    z3 = NY * SLOT
    out = {}
    own = {0: ("kv", 0), 1: ("z1m", 0), 7: ("z1p", 0), 2: ("z2m", 0), 6: ("z2p", 0), 3: ("s1m", z3), 5: ("s1p", z3), 4: ("s2p", z3)}
    side = {0: ("g0", 0), 1: ("ga", 0), 7: ("ga", 1), 2: ("ga", 2), 6: ("ga", 3), 3: ("gb", 0), 5: ("gb", 1), 4: ("gc", 0)}
    far = {0: ("gbm", 2), 1: ("gbp", 2), 7: ("gbp", 3), 2: ("gcp", 1), 6: ("gcm", 1), 3: ("gcp", 2), 5: ("gcm", 2), 4: ("gdp", 0)}
    for dz in range(NZ):
        out[0, dz] = own[dz]
        out[2, dz] = far[dz][0], far[dz][1] * ZROWS
        for dy, way in ((3, "p"), (1, "m")):
            out[dy, dz] = side[dz][0] + way, side[dz][1] * ZROWS
    return out


def gather(kv, w, turn, early):
    half = ZROWS + LAST // 2
    z1p, z1m, g0p, g0m = zp(kv), zm(kv), yp(kv), ym(kv)
    w = lax.ppermute(w, AXES, turn)
    (z1p, z1m, g0p, g0m, w), early = gate((z1p, z1m, g0p, g0m, w), early)
    to_p, to_m, w2, z2p, z2m = join(g0p[ZROWS:half], w), join(g0m[half:], w), y2(w), zp(z1p), zm(z1m)
    both_p, both_m = yp(to_p), ym(to_m)
    (both_p, both_m, w2, z2p, z2m), _ = gate((both_p, both_m, w2, z2p, z2m), ())
    n = LAST // 2
    s0 = kv[ZROWS:], w, g0p[ZROWS:], both_p[n:], g0m[ZROWS:], both_m[n:], both_p[:n], both_m[:n], w2
    s0p, s0m, ga = join(*s0, z2p[:ZROWS]), join(*s0, z2m[:ZROWS]), join(*(v[:ZROWS] for v in (z1m, z1p, z2m, z2p)))
    s1p, s1m, gap, gam = zp(s0p), zm(s0m), yp(ga), ym(ga)
    (s1p, s1m, gap, gam), _ = gate((s1p, s1m, gap, gam), ())
    z3, chunk = NY * SLOT, lambda v, i: v[i * ZROWS : (i + 1) * ZROWS]
    z3m, z3p = s1m[z3:], s1p[z3:]
    s2p, s2m, gbp, gbm = zp(s1p), zm(s1m), yp(join(z3m, z3p, gap[: 2 * ZROWS])), ym(join(z3m, z3p, g0m[:ZROWS]))
    (s2p, s2m, gbp, gbm), _ = gate((s2p, s2m, gbp, gbm), ())
    z4 = s2p[z3:]
    s3p, s3m = zp(s2p[:z3]), zm(s2m[:z3])
    gcp, gcm = yp(join(z4, chunk(gap, 2), chunk(gbp, 0))), ym(join(z4, chunk(gam, 3), chunk(gbm, 1)))
    (s3p, s3m, gcp, gcm), _ = gate((s3p, s3m, gcp, gcm), ())
    s4p, s4m, gdp = zp(s3p[: z3 // 2]), zm(s3m[z3 // 2 :]), yp(chunk(gcp, 0))
    named = (kv, z1m, z1p, z2m, z2p, s1m, s1p, s2p, g0p, g0m, gap, gam, gbp, gbm, gcp, gcm, gdp)
    return named, [s0p, s1m, s2m, s3m, s4p, s3p, s2p, s1p, s4m], early


TILE = 128


def attend_kernel(route_ref, place_ref, table_ref, q_ref, k_ref, v_ref, *rest):
    count = len(ARRAYS)
    named, ya, out_ref, (kbuf, vbuf, sems) = rest[:count], rest[count : count + 9], rest[count + 9], rest[count + 10 :]
    n = HEADS * SLOTS
    y, z = place_ref[0], place_ref[1]
    me = y * NZ + z

    def copies(u, i, block, first):
        rows = lambda at, size: block.at[pl.ds(pl.multiple_of(first + at, 16), size)]
        part = lambda at, size: vbuf.at[u, pl.ds(at, size), pl.ds(0, HD)]
        if i == 1:
            return [pltpu.make_async_copy(rows(0, LAST), part(ZVALUES, LAST), sems.at[u, 2])]
        return [
            pltpu.make_async_copy(rows(0, BLK), kbuf.at[u], sems.at[u, 0]),
            pltpu.make_async_copy(rows(BLK, ZVALUES), part(0, ZVALUES), sems.at[u, 1]),
        ]

    def start(u, i, arrays, array, first, step):
        for low in range(0, len(arrays), step):

            @pl.when((array >= low) & (array < low + step))
            def _():
                for a in range(low, min(low + step, len(arrays))):

                    @pl.when(array == a)
                    def _():
                        for copy in copies(u, i, arrays[a], first):
                            copy.start()

    for u in range(n):
        j = route_ref[u]
        by, dz = j >> 3, (j - z) & (NZ - 1)
        dy = (by - y) & (NY - 1)
        code = table_ref[dy * NZ + dz]
        start(u, 0, named, code & 31, (code >> 5) * 16, 5)
        slot = jnp.where(dy == 0, 0, jnp.where(dy == 3, 1, jnp.where(dy == 1, 2, 3)))
        late = (dz == 4) & (slot >= 2)
        start(u, 1, ya, jnp.where(late, NZ, dz), jnp.where(late, slot - 2, slot) * SLOT, 3)

    for u in range(n + 1):
        vbuf[u, :, HD:] = jnp.ones((BLK, HD), jnp.bfloat16)
    vbuf[n, :, :HD] = v_ref[...]
    scores_of = lambda q, k: lax.dot_general(q, k, (((1,), (1,)), ((), ())), preferred_element_type=jnp.float32)
    for h in range(HEADS):
        cols = slice(h * HD, (h + 1) * HD)
        for s in range(SLOTS):
            u = h * SLOTS + s
            for i, arrays in enumerate((named, ya)):
                for copy in copies(u, i, arrays[0], 0):
                    copy.wait()
        for t in range(BLK // TILE):
            rows = slice(t * TILE, (t + 1) * TILE)
            q = q_ref[rows, cols]
            seen = (t + 1) * TILE
            own = scores_of(q, k_ref[:seen])
            later = lax.broadcasted_iota(jnp.int32, (TILE, seen), 1) - t * TILE
            own = jnp.where(lax.broadcasted_iota(jnp.int32, (TILE, seen), 0) >= later, own, -1e30)
            m = jnp.max(own, axis=1, keepdims=True) * SCALE
            scores = []
            for s in range(SLOTS):
                u = h * SLOTS + s
                sc = scores_of(q, kbuf[u])
                top = jnp.max(sc, axis=1, keepdims=True) * SCALE
                m = jnp.maximum(m, jnp.where(route_ref[u] < me, top, -1e30))
                scores.append(sc)
            e = jnp.exp2(own * SCALE - m).astype(jnp.bfloat16)
            both = jnp.dot(e, vbuf[n, :seen], preferred_element_type=jnp.float32)
            for s in range(SLOTS):
                u = h * SLOTS + s
                e = jnp.exp2(scores[s] * SCALE - jnp.where(route_ref[u] < me, m, 1e30)).astype(jnp.bfloat16)
                both = both + jnp.dot(e, vbuf[u], preferred_element_type=jnp.float32)
            out_ref[rows, cols] = (both[:, :HD] / both[:, HD:]).astype(out_ref.dtype)


def own_kernel(at_ref, a_ref, *rest):
    arrays, total_ref, near_ref, far_ref, buf, sems = rest[:9], rest[9], rest[10], rest[11], rest[12], rest[13]
    dests = (buf, near_ref.at[0], near_ref.at[1], far_ref)
    for i, dest in enumerate(dests):
        slot = at_ref[1 + i]
        for dz in range(NZ):
            col = (at_ref[0] + dz) & (NZ - 1)

            def copy(array, at):
                rows = pl.ds(pl.multiple_of(at * SLOT + LAST, 16), BLK)
                pltpu.make_async_copy(array.at[rows], dest.at[col], sems.at[i]).start()

            if dz == 4:
                pl.when(slot < 2)(lambda: copy(arrays[4], slot))
                pl.when(slot >= 2)(lambda: copy(arrays[8], slot - 2))
            else:
                copy(arrays[dz], slot)
    pltpu.make_async_copy(buf, buf, sems.at[0]).wait()
    for n in range(NZ // 2):
        cols = jnp.concatenate([buf[2 * n], buf[2 * n + 1]], axis=1)
        total_ref[:, n * 2 * HD : (n + 1) * 2 * HD] = jnp.dot(a_ref[...], cols, preferred_element_type=jnp.float32)
    for i, dest in enumerate(dests[1:]):
        pltpu.make_async_copy(dest, dest, sems.at[1 + i]).wait()


def near_kernel(total_ref, a0_ref, a1_ref, w_ref, out_ref):
    for n in range(NZ // 2):
        cols = slice(n * 2 * HD, (n + 1) * 2 * HD)
        total = total_ref[:, cols]
        for i, a_ref in enumerate((a0_ref, a1_ref)):
            rows = jnp.concatenate([w_ref[i, 2 * n], w_ref[i, 2 * n + 1]], axis=1)
            total = total + jnp.dot(a_ref[...], rows, preferred_element_type=jnp.float32)
        out_ref[:, cols] = total


def far_kernel(core_ref, total_ref, a0_ref, a1_ref, w_ref, out_ref):
    width, count = NZ * HD // NC, NZ // NC
    core = core_ref[0]
    for i, a_ref in enumerate((a0_ref, a1_ref)):
        rows = slice(i * HALF, (i + 1) * HALF)
        for n in range(count // 2):
            right = jnp.concatenate([w_ref[core * count + 2 * n], w_ref[core * count + 2 * n + 1]], axis=1)
            part = jnp.dot(a_ref[...], right, preferred_element_type=jnp.float32)
            cols = pl.ds(pl.multiple_of(core * width, width) + n * 2 * HD, 2 * HD)
            out_ref[rows, n * 2 * HD : (n + 1) * 2 * HD] = (total_ref[rows, cols] + part).astype(out_ref.dtype)


def call(kernel, out_shape, scalars, near, far, scratch, flops, exps=0, vmem=32):
    spec = lambda space, arrays: [pl.BlockSpec(memory_space=space)] * len(arrays)
    return pl.pallas_call(
        kernel,
        out_shape=out_shape,
        in_specs=spec(pltpu.SMEM, scalars) + spec(pltpu.VMEM, near) + spec(pl.ANY, far),
        out_specs=jax.tree.map(lambda _: pl.BlockSpec(memory_space=pltpu.VMEM), out_shape),
        scratch_shapes=scratch,
        compiler_params=pltpu.CompilerParams(vmem_limit_bytes=vmem << 20),
        cost_estimate=pl.CostEstimate(flops=flops, transcendentals=exps, bytes_accessed=8 << 20),
    )(*scalars, *near, *far)


def attention(route, place, q, k, v, named, ya):
    n = HEADS * SLOTS
    table = [0] * (NY * NZ)
    for (dy, dz), (name, first) in places().items():
        table[dy * NZ + dz] = ARRAYS.index(name) + first // 16 * 32
    scratch = [
        pltpu.VMEM((n, BLK, HD), jnp.bfloat16),
        pltpu.VMEM((n + 1, BLK, 2 * HD), jnp.bfloat16),
        pltpu.SemaphoreType.DMA((n, 3)),
    ]
    out = jax.ShapeDtypeStruct((BLK, HEADS * HD), jnp.bfloat16)
    flops, exps = 6 * (n + HEADS) * BLK * BLK * HD, (n + HEADS) * BLK * BLK
    scalars = (route, place, jnp.asarray(table, jnp.int32))
    return call(attend_kernel, out, scalars, (q, k, v), (*named, *ya), scratch, flops, exps, 56)


def project_own(at, a, w):
    total = jax.ShapeDtypeStruct((BLK, NZ * HD), jnp.float32)
    rows = lambda *n: jax.ShapeDtypeStruct((*n, NZ, BLK, HD), jnp.bfloat16)
    scratch = [pltpu.VMEM((NZ, BLK, HD), jnp.bfloat16), pltpu.SemaphoreType.DMA((4,))]
    return call(own_kernel, (total, rows(2), rows()), (at,), (a,), w, scratch, 2 * BLK * BLK * NZ * HD, vmem=56)


def project_near(total, a0, a1, w):
    out = jax.ShapeDtypeStruct((BLK, NZ * HD), jnp.float32)
    return call(near_kernel, out, (), (total, a0, a1, w), (), (), 4 * BLK * BLK * NZ * HD)


def project_far(core, total, a0, a1, w, dtype):
    out = jax.ShapeDtypeStruct((BLK, NZ * HD // NC), dtype)
    return call(far_kernel, out, (core[None],), (total, a0, a1, w), (), (), 2 * BLK * BLK * NZ * HD // NC)


def body(queries, keys, values, routing, w_out):
    y, z, x, c = (lax.axis_index(a) for a in AXES)
    at = lambda y, z, x, c: ((y * NZ + z) * NX + x) * NC + c
    turn = [
        (at(y, z, x, c), at(x, z, y, c)) for y in range(NY) for z in range(NZ) for x in range(NX) for c in range(NC)
    ]
    route = lax.dynamic_index_in_dim(routing, y * NZ + z, 0, keepdims=False).reshape(-1)

    def rows_of(x):
        d = (x - y) % NX
        return jnp.where(d == 0, 0, jnp.where(d == 3, 1, jnp.where(d == 1, 2, 3)))

    at = jnp.stack([z] + [rows_of(x + d) for d in (0, -1, 1, 2)])
    named, ya, (route, at) = gather(join(keys, values), w_out, turn, (route, at))
    attn = attention(route, jnp.stack([y, z]), queries, keys, values, named, ya)
    x1p, x1m = xp(attn), xm(attn)
    (x1p, x1m), (total, near, far) = gate((x1p, x1m), project_own(at, attn, ya))
    x2p, x2m = xp(x1p[:HALF]), xm(x1m[HALF:])
    total = project_near(total, x1p, x1m, near)
    theirs = swap(project_far(1 - c, total, x2p, x2m, far, jnp.bfloat16))
    mine = project_far(c, total, x2p, x2m, far, jnp.float32)
    return (mine + theirs.astype(jnp.float32)).astype(jnp.bfloat16)


def solution(mesh):
    grid = Mesh(mesh.devices.reshape(NY, NZ, NX, NC), AXES)
    seq, mp = ("y", "z"), ("x", "c")
    in_specs = (P(seq, mp), P(seq, mp), P(seq, mp), P(None, mp, None), P(mp, seq))
    return jax.shard_map(body, mesh=grid, in_specs=in_specs, out_specs=P(seq, mp), check_vma=False)
```

```python
import functools
import math

import jax
import jax.numpy as jnp
from jax import lax
from jax.experimental import pallas as pl
from jax.experimental.pallas import tpu as pltpu
from jax.sharding import Mesh, PartitionSpec as P

HD = 128
BLK = 512
HEADS = 4
SLOTS = 3
NY, NZ, NX, NC = 4, 8, 4, 2
AXES = ("y", "z", "x", "c")
ARRAYS = ("kv", "z1m", "z1p", "z2m", "z2p", "s1m", "s1p", "s2p", "g0p", "g0m")
ARRAYS += ("gap", "gam", "gbp", "gbm", "gcp", "gcm", "gdp")
HALF = BLK // 2
ZROWS = 896
ZVALUES = ZROWS - BLK
LAST = BLK - ZVALUES
SLOT = LAST + BLK
SCALE = math.log2(math.e) / math.sqrt(HD)
def shift(v, axis, d, n):
    return lax.ppermute(v, axis, [(i, (i + d) % n) for i in range(n)])


zp = functools.partial(shift, axis="z", d=1, n=NZ)
zm = functools.partial(shift, axis="z", d=-1, n=NZ)
yp = functools.partial(shift, axis="y", d=1, n=NY)
ym = functools.partial(shift, axis="y", d=-1, n=NY)
y2 = functools.partial(shift, axis="y", d=2, n=NY)
xp = functools.partial(shift, axis="x", d=1, n=NX)
xm = functools.partial(shift, axis="x", d=-1, n=NX)
swap = functools.partial(shift, axis="c", d=1, n=NC)


def gate(vals, waits):
    return lax.optimization_barrier((vals, waits))


def join(*parts):
    return jnp.concatenate(parts)


def places():
    z3 = NY * SLOT
    out = {}
    own = {0: ("kv", 0), 1: ("z1m", 0), 7: ("z1p", 0), 2: ("z2m", 0), 6: ("z2p", 0), 3: ("s1m", z3), 5: ("s1p", z3), 4: ("s2p", z3)}
    side = {0: ("g0", 0), 1: ("ga", 0), 7: ("ga", 1), 2: ("ga", 2), 6: ("ga", 3), 3: ("gb", 0), 5: ("gb", 1), 4: ("gc", 0)}
    far = {0: ("gbm", 2), 1: ("gbp", 2), 7: ("gbp", 3), 2: ("gcp", 1), 6: ("gcm", 1), 3: ("gcp", 2), 5: ("gcm", 2), 4: ("gdp", 0)}
    for dz in range(NZ):
        out[0, dz] = own[dz]
        out[2, dz] = far[dz][0], far[dz][1] * ZROWS
        for dy, way in ((3, "p"), (1, "m")):
            out[dy, dz] = side[dz][0] + way, side[dz][1] * ZROWS
    return out


def gather(kv, w, turn, early):
    half = ZROWS + LAST // 2
    z1p, z1m, g0p, g0m = zp(kv), zm(kv), yp(kv), ym(kv)
    w = lax.ppermute(w, AXES, turn)
    (z1p, z1m, g0p, g0m, w), early = gate((z1p, z1m, g0p, g0m, w), early)
    to_p, to_m, w2, z2p, z2m = join(g0p[ZROWS:half], w), join(g0m[half:], w), y2(w), zp(z1p), zm(z1m)
    both_p, both_m = yp(to_p), ym(to_m)
    (both_p, both_m, w2, z2p, z2m), _ = gate((both_p, both_m, w2, z2p, z2m), ())
    n = LAST // 2
    s0 = kv[ZROWS:], w, g0p[ZROWS:], both_p[n:], g0m[ZROWS:], both_m[n:], both_p[:n], both_m[:n], w2
    s0p, s0m, ga = join(*s0, z2p[:ZROWS]), join(*s0, z2m[:ZROWS]), join(*(v[:ZROWS] for v in (z1m, z1p, z2m, z2p)))
    s1p, s1m, gap, gam = zp(s0p), zm(s0m), yp(ga), ym(ga)
    (s1p, s1m, gap, gam), _ = gate((s1p, s1m, gap, gam), ())
    z3, chunk = NY * SLOT, lambda v, i: v[i * ZROWS : (i + 1) * ZROWS]
    z3m, z3p = s1m[z3:], s1p[z3:]
    s2p, s2m, gbp, gbm = zp(s1p), zm(s1m), yp(join(z3m, z3p, gap[: 2 * ZROWS])), ym(join(z3m, z3p, g0m[:ZROWS]))
    (s2p, s2m, gbp, gbm), _ = gate((s2p, s2m, gbp, gbm), ())
    z4 = s2p[z3:]
    s3p, s3m = zp(s2p[:z3]), zm(s2m[:z3])
    gcp, gcm = yp(join(z4, chunk(gap, 2), chunk(gbp, 0))), ym(join(z4, chunk(gam, 3), chunk(gbm, 1)))
    (s3p, s3m, gcp, gcm), _ = gate((s3p, s3m, gcp, gcm), ())
    s4p, s4m, gdp = zp(s3p[: z3 // 2]), zm(s3m[z3 // 2 :]), yp(chunk(gcp, 0))
    named = (kv, z1m, z1p, z2m, z2p, s1m, s1p, s2p, g0p, g0m, gap, gam, gbp, gbm, gcp, gcm, gdp)
    return named, [s0p, s1m, s2m, s3m, s4p, s3p, s2p, s1p, s4m], early


TILE = 128


def attend_kernel(route_ref, place_ref, table_ref, q_ref, k_ref, v_ref, *rest):
    count = len(ARRAYS)
    named, ya, out_ref, (kbuf, vbuf, sems) = rest[:count], rest[count : count + 9], rest[count + 9], rest[count + 10 :]
    n = HEADS * SLOTS
    y, z = place_ref[0], place_ref[1]
    me = y * NZ + z

    def copies(u, i, block, first):
        rows = lambda at, size: block.at[pl.ds(pl.multiple_of(first + at, 16), size)]
        part = lambda at, size: vbuf.at[u, pl.ds(at, size), pl.ds(0, HD)]
        if i == 1:
            return [pltpu.make_async_copy(rows(0, LAST), part(ZVALUES, LAST), sems.at[u, 2])]
        return [
            pltpu.make_async_copy(rows(0, BLK), kbuf.at[u], sems.at[u, 0]),
            pltpu.make_async_copy(rows(BLK, ZVALUES), part(0, ZVALUES), sems.at[u, 1]),
        ]

    def start(u, i, arrays, array, first, step):
        for low in range(0, len(arrays), step):

            @pl.when((array >= low) & (array < low + step))
            def _():
                for a in range(low, min(low + step, len(arrays))):

                    @pl.when(array == a)
                    def _():
                        for copy in copies(u, i, arrays[a], first):
                            copy.start()

    for u in range(n):
        j = route_ref[u]
        by, dz = j >> 3, (j - z) & (NZ - 1)
        dy = (by - y) & (NY - 1)
        code = table_ref[dy * NZ + dz]
        start(u, 0, named, code & 31, (code >> 5) * 16, 5)
        slot = jnp.where(dy == 0, 0, jnp.where(dy == 3, 1, jnp.where(dy == 1, 2, 3)))
        late = (dz == 4) & (slot >= 2)
        start(u, 1, ya, jnp.where(late, NZ, dz), jnp.where(late, slot - 2, slot) * SLOT, 3)

    for u in range(n + 1):
        vbuf[u, :, HD:] = jnp.ones((BLK, HD), jnp.bfloat16)
    vbuf[n, :, :HD] = v_ref[...]
    scores_of = lambda q, k: lax.dot_general(q, k, (((1,), (1,)), ((), ())), preferred_element_type=jnp.float32)
    for h in range(HEADS):
        cols = slice(h * HD, (h + 1) * HD)
        for s in range(SLOTS):
            u = h * SLOTS + s
            for i, arrays in enumerate((named, ya)):
                for copy in copies(u, i, arrays[0], 0):
                    copy.wait()
        for t in range(BLK // TILE):
            rows = slice(t * TILE, (t + 1) * TILE)
            q = q_ref[rows, cols]
            seen = (t + 1) * TILE
            own = scores_of(q, k_ref[:seen])
            later = lax.broadcasted_iota(jnp.int32, (TILE, seen), 1) - t * TILE
            own = jnp.where(lax.broadcasted_iota(jnp.int32, (TILE, seen), 0) >= later, own, -1e30)
            m = jnp.max(own, axis=1, keepdims=True) * SCALE
            scores = []
            for s in range(SLOTS):
                u = h * SLOTS + s
                sc = scores_of(q, kbuf[u])
                top = jnp.max(sc, axis=1, keepdims=True) * SCALE
                m = jnp.maximum(m, jnp.where(route_ref[u] < me, top, -1e30))
                scores.append(sc)
            e = jnp.exp2(own * SCALE - m).astype(jnp.bfloat16)
            both = jnp.dot(e, vbuf[n, :seen], preferred_element_type=jnp.float32)
            for s in range(SLOTS):
                u = h * SLOTS + s
                e = jnp.exp2(scores[s] * SCALE - jnp.where(route_ref[u] < me, m, 1e30)).astype(jnp.bfloat16)
                both = both + jnp.dot(e, vbuf[u], preferred_element_type=jnp.float32)
            out_ref[rows, cols] = (both[:, :HD] / both[:, HD:]).astype(out_ref.dtype)


def own_kernel(at_ref, a_ref, *rest):
    arrays, total_ref, near_ref, far_ref, buf, sems = rest[:9], rest[9], rest[10], rest[11], rest[12], rest[13]
    dests = (buf, near_ref.at[0], near_ref.at[1], far_ref)
    for i, dest in enumerate(dests):
        slot = at_ref[1 + i]
        for dz in range(NZ):
            col = (at_ref[0] + dz) & (NZ - 1)

            def copy(array, at):
                rows = pl.ds(pl.multiple_of(at * SLOT + LAST, 16), BLK)
                pltpu.make_async_copy(array.at[rows], dest.at[col], sems.at[i]).start()

            if dz == 4:
                pl.when(slot < 2)(lambda: copy(arrays[4], slot))
                pl.when(slot >= 2)(lambda: copy(arrays[8], slot - 2))
            else:
                copy(arrays[dz], slot)
    pltpu.make_async_copy(buf, buf, sems.at[0]).wait()
    for n in range(NZ // 2):
        cols = jnp.concatenate([buf[2 * n], buf[2 * n + 1]], axis=1)
        total_ref[:, n * 2 * HD : (n + 1) * 2 * HD] = jnp.dot(a_ref[...], cols, preferred_element_type=jnp.float32)
    for i, dest in enumerate(dests[1:]):
        pltpu.make_async_copy(dest, dest, sems.at[1 + i]).wait()


def near_kernel(total_ref, a0_ref, a1_ref, w_ref, out_ref):
    for n in range(NZ // 2):
        cols = slice(n * 2 * HD, (n + 1) * 2 * HD)
        total = total_ref[:, cols]
        for i, a_ref in enumerate((a0_ref, a1_ref)):
            rows = jnp.concatenate([w_ref[i, 2 * n], w_ref[i, 2 * n + 1]], axis=1)
            total = total + jnp.dot(a_ref[...], rows, preferred_element_type=jnp.float32)
        out_ref[:, cols] = total


def far_kernel(core_ref, total_ref, a0_ref, a1_ref, w_ref, out_ref):
    width, count = NZ * HD // NC, NZ // NC
    core = core_ref[0]
    for i, a_ref in enumerate((a0_ref, a1_ref)):
        rows = slice(i * HALF, (i + 1) * HALF)
        for n in range(count // 2):
            right = jnp.concatenate([w_ref[core * count + 2 * n], w_ref[core * count + 2 * n + 1]], axis=1)
            part = jnp.dot(a_ref[...], right, preferred_element_type=jnp.float32)
            cols = pl.ds(pl.multiple_of(core * width, width) + n * 2 * HD, 2 * HD)
            out_ref[rows, n * 2 * HD : (n + 1) * 2 * HD] = (total_ref[rows, cols] + part).astype(out_ref.dtype)


def call(kernel, out_shape, scalars, near, far, scratch, flops, exps=0, vmem=32):
    spec = lambda space, arrays: [pl.BlockSpec(memory_space=space)] * len(arrays)
    return pl.pallas_call(
        kernel,
        out_shape=out_shape,
        in_specs=spec(pltpu.SMEM, scalars) + spec(pltpu.VMEM, near) + spec(pl.ANY, far),
        out_specs=jax.tree.map(lambda _: pl.BlockSpec(memory_space=pltpu.VMEM), out_shape),
        scratch_shapes=scratch,
        compiler_params=pltpu.CompilerParams(vmem_limit_bytes=vmem << 20),
        cost_estimate=pl.CostEstimate(flops=flops, transcendentals=exps, bytes_accessed=8 << 20),
    )(*scalars, *near, *far)


def attention(route, place, q, k, v, named, ya):
    n = HEADS * SLOTS
    table = [0] * (NY * NZ)
    for (dy, dz), (name, first) in places().items():
        table[dy * NZ + dz] = ARRAYS.index(name) + first // 16 * 32
    scratch = [
        pltpu.VMEM((n, BLK, HD), jnp.bfloat16),
        pltpu.VMEM((n + 1, BLK, 2 * HD), jnp.bfloat16),
        pltpu.SemaphoreType.DMA((n, 3)),
    ]
    out = jax.ShapeDtypeStruct((BLK, HEADS * HD), jnp.bfloat16)
    flops, exps = 6 * (n + HEADS) * BLK * BLK * HD, (n + HEADS) * BLK * BLK
    scalars = (route, place, jnp.asarray(table, jnp.int32))
    return call(attend_kernel, out, scalars, (q, k, v), (*named, *ya), scratch, flops, exps, 56)


def project_own(at, a, w):
    total = jax.ShapeDtypeStruct((BLK, NZ * HD), jnp.float32)
    rows = lambda *n: jax.ShapeDtypeStruct((*n, NZ, BLK, HD), jnp.bfloat16)
    scratch = [pltpu.VMEM((NZ, BLK, HD), jnp.bfloat16), pltpu.SemaphoreType.DMA((4,))]
    return call(own_kernel, (total, rows(2), rows()), (at,), (a,), w, scratch, 2 * BLK * BLK * NZ * HD, vmem=56)


def project_near(total, a0, a1, w):
    out = jax.ShapeDtypeStruct((BLK, NZ * HD), jnp.float32)
    return call(near_kernel, out, (), (total, a0, a1, w), (), (), 4 * BLK * BLK * NZ * HD)


def project_far(core, total, a0, a1, w, dtype):
    out = jax.ShapeDtypeStruct((BLK, NZ * HD // NC), dtype)
    return call(far_kernel, out, (core[None],), (total, a0, a1, w), (), (), 2 * BLK * BLK * NZ * HD // NC)


def body(queries, keys, values, routing, w_out):
    y, z, x, c = (lax.axis_index(a) for a in AXES)
    at = lambda y, z, x, c: ((y * NZ + z) * NX + x) * NC + c
    turn = [
        (at(y, z, x, c), at(x, z, y, c)) for y in range(NY) for z in range(NZ) for x in range(NX) for c in range(NC)
    ]
    route = lax.dynamic_index_in_dim(routing, y * NZ + z, 0, keepdims=False).reshape(-1)

    def rows_of(x):
        d = (x - y) % NX
        return jnp.where(d == 0, 0, jnp.where(d == 3, 1, jnp.where(d == 1, 2, 3)))

    at = jnp.stack([z] + [rows_of(x + d) for d in (0, -1, 1, 2)])
    named, ya, (route, at) = gather(jnp.stack([keys, values]).reshape(2 * BLK, HD), w_out, turn, (route, at))
    attn = attention(route, jnp.stack([y, z]), queries, keys, values, named, ya)
    x1p, x1m = xp(attn), xm(attn)
    (x1p, x1m), (total, near, far) = gate((x1p, x1m), project_own(at, attn, ya))
    x2p, x2m = xp(x1p[:HALF]), xm(x1m[HALF:])
    total = project_near(total, x1p, x1m, near)
    theirs = swap(project_far(1 - c, total, x2p, x2m, far, jnp.bfloat16))
    mine = project_far(c, total, x2p, x2m, far, jnp.float32)
    return (mine + theirs.astype(jnp.float32)).astype(jnp.bfloat16)


def solution(mesh):
    grid = Mesh(mesh.devices.reshape(NY, NZ, NX, NC), AXES)
    seq, mp = ("y", "z"), ("x", "c")
    in_specs = (P(seq, mp), P(seq, mp), P(seq, mp), P(None, mp, None), P(mp, seq))
    return jax.shard_map(body, mesh=grid, in_specs=in_specs, out_specs=P(seq, mp), check_vma=False)
```

```python
import functools
import math

import jax
import jax.numpy as jnp
from jax import lax
from jax.experimental import pallas as pl
from jax.experimental.pallas import tpu as pltpu
from jax.sharding import Mesh, PartitionSpec as P

HD = 128
BLK = 512
HEADS = 4
SLOTS = 3
NY, NZ, NX, NC = 4, 8, 4, 2
AXES = ("y", "z", "x", "c")
ARRAYS = ("kv", "z1m", "z1p", "z2m", "z2p", "s1m", "s1p", "s2p", "g0p", "g0m")
ARRAYS += ("gap", "gam", "gbp", "gbm", "gcp", "gcm", "gdp")
HALF = BLK // 2
ZROWS = 896
ZVALUES = ZROWS - BLK
LAST = BLK - ZVALUES
SLOT = LAST + BLK
SCALE = math.log2(math.e) / math.sqrt(HD)
def shift(v, axis, d, n):
    return lax.ppermute(v, axis, [(i, (i + d) % n) for i in range(n)])


zp = functools.partial(shift, axis="z", d=1, n=NZ)
zm = functools.partial(shift, axis="z", d=-1, n=NZ)
yp = functools.partial(shift, axis="y", d=1, n=NY)
ym = functools.partial(shift, axis="y", d=-1, n=NY)
y2 = functools.partial(shift, axis="y", d=2, n=NY)
xp = functools.partial(shift, axis="x", d=1, n=NX)
xm = functools.partial(shift, axis="x", d=-1, n=NX)
swap = functools.partial(shift, axis="c", d=1, n=NC)


def gate(vals, waits):
    return lax.optimization_barrier((vals, waits))


def join(*parts):
    return jnp.concatenate(parts)


def places():
    z3 = NY * SLOT
    out = {}
    own = {0: ("kv", 0), 1: ("z1m", 0), 7: ("z1p", 0), 2: ("z2m", 0), 6: ("z2p", 0), 3: ("s1m", z3), 5: ("s1p", z3), 4: ("s2p", z3)}
    side = {0: ("g0", 0), 1: ("ga", 0), 7: ("ga", 1), 2: ("ga", 2), 6: ("ga", 3), 3: ("gb", 0), 5: ("gb", 1), 4: ("gc", 0)}
    far = {0: ("gbm", 2), 1: ("gbp", 2), 7: ("gbp", 3), 2: ("gcp", 1), 6: ("gcm", 1), 3: ("gcp", 2), 5: ("gcm", 2), 4: ("gdp", 0)}
    for dz in range(NZ):
        out[0, dz] = own[dz]
        out[2, dz] = far[dz][0], far[dz][1] * ZROWS
        for dy, way in ((3, "p"), (1, "m")):
            out[dy, dz] = side[dz][0] + way, side[dz][1] * ZROWS
    return out


def gather(kv, w, turn, early):
    half = ZROWS + LAST // 2
    z1p, z1m, g0p, g0m = zp(kv), zm(kv), yp(kv), ym(kv)
    w = lax.ppermute(w, AXES, turn)
    (z1p, z1m, g0p, g0m, w), early = gate((z1p, z1m, g0p, g0m, w), early)
    to_p, to_m, w2, z2p, z2m = join(g0p[ZROWS:half], w), join(g0m[half:], w), y2(w), zp(z1p), zm(z1m)
    both_p, both_m = yp(to_p), ym(to_m)
    (both_p, both_m, w2, z2p, z2m), _ = gate((both_p, both_m, w2, z2p, z2m), ())
    n = LAST // 2
    s0 = kv[ZROWS:], w, g0p[ZROWS:], both_p[n:], g0m[ZROWS:], both_m[n:], both_p[:n], both_m[:n], w2
    s0p, s0m, ga = join(*s0, z2p[:ZROWS]), join(*s0, z2m[:ZROWS]), join(*(v[:ZROWS] for v in (z1m, z1p, z2m, z2p)))
    s1p, s1m, gap, gam = zp(s0p), zm(s0m), yp(ga), ym(ga)
    (s1p, s1m, gap, gam), _ = gate((s1p, s1m, gap, gam), ())
    z3, chunk = NY * SLOT, lambda v, i: v[i * ZROWS : (i + 1) * ZROWS]
    z3m, z3p = s1m[z3:], s1p[z3:]
    s2p, s2m, gbp, gbm = zp(s1p), zm(s1m), yp(join(z3m, z3p, gap[: 2 * ZROWS])), ym(join(z3m, z3p, g0m[:ZROWS]))
    (s2p, s2m, gbp, gbm), _ = gate((s2p, s2m, gbp, gbm), ())
    z4 = s2p[z3:]
    s3p, s3m = zp(s2p[:z3]), zm(s2m[:z3])
    gcp, gcm = yp(join(z4, chunk(gap, 2), chunk(gbp, 0))), ym(join(z4, chunk(gam, 3), chunk(gbm, 1)))
    (s3p, s3m, gcp, gcm), _ = gate((s3p, s3m, gcp, gcm), ())
    slots = lambda v, two, first, size: join(*(v[i * SLOT + first : i * SLOT + first + size] for i in two))
    v4p, v4m, gdp = zp(slots(s3p, (0, 1), 0, LAST)), zm(slots(s3m, (2, 3), 0, LAST)), yp(chunk(gcp, 0))
    w4p, w4m = zp(slots(s3p, (0, 1), LAST, BLK)), zm(slots(s3m, (2, 3), LAST, BLK))
    named = (kv, z1m, z1p, z2m, z2p, s1m, s1p, s2p, g0p, g0m, gap, gam, gbp, gbm, gcp, gcm, gdp)
    ring = lambda p, m: [s0p, s1m, s2m, s3m, p, s3p, s2p, s1p, m]
    return named, ring(v4p, v4m), ring(w4p, w4m), early


TILE = 128


def attend_kernel(route_ref, place_ref, table_ref, q_ref, k_ref, v_ref, *rest):
    count = len(ARRAYS)
    named, ya, out_ref, (kbuf, vbuf, sems) = rest[:count], rest[count : count + 9], rest[count + 9], rest[count + 10 :]
    n = HEADS * SLOTS
    y, z = place_ref[0], place_ref[1]
    me = y * NZ + z

    def copies(u, i, block, first):
        rows = lambda at, size: block.at[pl.ds(pl.multiple_of(first + at, 16), size)]
        part = lambda at, size: vbuf.at[u, pl.ds(at, size), pl.ds(0, HD)]
        if i == 1:
            return [pltpu.make_async_copy(rows(0, LAST), part(ZVALUES, LAST), sems.at[u, 2])]
        return [
            pltpu.make_async_copy(rows(0, BLK), kbuf.at[u], sems.at[u, 0]),
            pltpu.make_async_copy(rows(BLK, ZVALUES), part(0, ZVALUES), sems.at[u, 1]),
        ]

    def start(u, i, arrays, array, first, step):
        for low in range(0, len(arrays), step):

            @pl.when((array >= low) & (array < low + step))
            def _():
                for a in range(low, min(low + step, len(arrays))):

                    @pl.when(array == a)
                    def _():
                        for copy in copies(u, i, arrays[a], first):
                            copy.start()

    for u in range(n):
        j = route_ref[u]
        by, dz = j >> 3, (j - z) & (NZ - 1)
        dy = (by - y) & (NY - 1)
        code = table_ref[dy * NZ + dz]
        start(u, 0, named, code & 31, (code >> 5) * 16, 5)
        slot = jnp.where(dy == 0, 0, jnp.where(dy == 3, 1, jnp.where(dy == 1, 2, 3)))
        late = (dz == 4) & (slot >= 2)
        start(u, 1, ya, jnp.where(late, NZ, dz), jnp.where(late, slot - 2, slot) * jnp.where(dz == 4, LAST, SLOT), 3)

    for u in range(n + 1):
        vbuf[u, :, HD:] = jnp.ones((BLK, HD), jnp.bfloat16)
    vbuf[n, :, :HD] = v_ref[...]
    scores_of = lambda q, k: lax.dot_general(q, k, (((1,), (1,)), ((), ())), preferred_element_type=jnp.float32)
    for h in range(HEADS):
        cols = slice(h * HD, (h + 1) * HD)
        for s in range(SLOTS):
            u = h * SLOTS + s
            for i, arrays in enumerate((named, ya)):
                for copy in copies(u, i, arrays[0], 0):
                    copy.wait()
        for t in range(BLK // TILE):
            rows = slice(t * TILE, (t + 1) * TILE)
            q = q_ref[rows, cols]
            seen = (t + 1) * TILE
            own = scores_of(q, k_ref[:seen])
            later = lax.broadcasted_iota(jnp.int32, (TILE, seen), 1) - t * TILE
            own = jnp.where(lax.broadcasted_iota(jnp.int32, (TILE, seen), 0) >= later, own, -1e30)
            m = jnp.max(own, axis=1, keepdims=True) * SCALE
            scores = []
            for s in range(SLOTS):
                u = h * SLOTS + s
                sc = scores_of(q, kbuf[u])
                top = jnp.max(sc, axis=1, keepdims=True) * SCALE
                m = jnp.maximum(m, jnp.where(route_ref[u] < me, top, -1e30))
                scores.append(sc)
            e = jnp.exp2(own * SCALE - m).astype(jnp.bfloat16)
            both = jnp.dot(e, vbuf[n, :seen], preferred_element_type=jnp.float32)
            for s in range(SLOTS):
                u = h * SLOTS + s
                e = jnp.exp2(scores[s] * SCALE - jnp.where(route_ref[u] < me, m, 1e30)).astype(jnp.bfloat16)
                both = both + jnp.dot(e, vbuf[u], preferred_element_type=jnp.float32)
            out_ref[rows, cols] = (both[:, :HD] / both[:, HD:]).astype(out_ref.dtype)


def own_kernel(at_ref, a_ref, *rest):
    arrays, total_ref, near_ref, far_ref, buf, sems = rest[:9], rest[9], rest[10], rest[11], rest[12], rest[13]
    dests = (buf, near_ref.at[0], near_ref.at[1], far_ref)
    for i, dest in enumerate(dests):
        slot = at_ref[1 + i]
        for dz in range(NZ):
            col = (at_ref[0] + dz) & (NZ - 1)

            def copy(array, at):
                rows = pl.ds(pl.multiple_of(at * BLK if dz == 4 else at * SLOT + LAST, 16), BLK)
                pltpu.make_async_copy(array.at[rows], dest.at[col], sems.at[i]).start()

            if dz == 4:
                pl.when(slot < 2)(lambda: copy(arrays[4], slot))
                pl.when(slot >= 2)(lambda: copy(arrays[8], slot - 2))
            else:
                copy(arrays[dz], slot)
    pltpu.make_async_copy(buf, buf, sems.at[0]).wait()
    for n in range(NZ // 2):
        cols = jnp.concatenate([buf[2 * n], buf[2 * n + 1]], axis=1)
        total_ref[:, n * 2 * HD : (n + 1) * 2 * HD] = jnp.dot(a_ref[...], cols, preferred_element_type=jnp.float32)
    for i, dest in enumerate(dests[1:]):
        pltpu.make_async_copy(dest, dest, sems.at[1 + i]).wait()


def near_kernel(total_ref, a0_ref, a1_ref, w_ref, out_ref):
    for n in range(NZ // 2):
        cols = slice(n * 2 * HD, (n + 1) * 2 * HD)
        total = total_ref[:, cols]
        for i, a_ref in enumerate((a0_ref, a1_ref)):
            rows = jnp.concatenate([w_ref[i, 2 * n], w_ref[i, 2 * n + 1]], axis=1)
            total = total + jnp.dot(a_ref[...], rows, preferred_element_type=jnp.float32)
        out_ref[:, cols] = total


def far_kernel(core_ref, total_ref, a0_ref, a1_ref, w_ref, out_ref):
    width, count = NZ * HD // NC, NZ // NC
    core = core_ref[0]
    for i, a_ref in enumerate((a0_ref, a1_ref)):
        rows = slice(i * HALF, (i + 1) * HALF)
        for n in range(count // 2):
            right = jnp.concatenate([w_ref[core * count + 2 * n], w_ref[core * count + 2 * n + 1]], axis=1)
            part = jnp.dot(a_ref[...], right, preferred_element_type=jnp.float32)
            cols = pl.ds(pl.multiple_of(core * width, width) + n * 2 * HD, 2 * HD)
            out_ref[rows, n * 2 * HD : (n + 1) * 2 * HD] = (total_ref[rows, cols] + part).astype(out_ref.dtype)


def call(kernel, out_shape, scalars, near, far, scratch, flops, exps=0, vmem=32):
    spec = lambda space, arrays: [pl.BlockSpec(memory_space=space)] * len(arrays)
    return pl.pallas_call(
        kernel,
        out_shape=out_shape,
        in_specs=spec(pltpu.SMEM, scalars) + spec(pltpu.VMEM, near) + spec(pl.ANY, far),
        out_specs=jax.tree.map(lambda _: pl.BlockSpec(memory_space=pltpu.VMEM), out_shape),
        scratch_shapes=scratch,
        compiler_params=pltpu.CompilerParams(vmem_limit_bytes=vmem << 20),
        cost_estimate=pl.CostEstimate(flops=flops, transcendentals=exps, bytes_accessed=8 << 20),
    )(*scalars, *near, *far)


def attention(route, place, q, k, v, named, ya):
    n = HEADS * SLOTS
    table = [0] * (NY * NZ)
    for (dy, dz), (name, first) in places().items():
        table[dy * NZ + dz] = ARRAYS.index(name) + first // 16 * 32
    scratch = [
        pltpu.VMEM((n, BLK, HD), jnp.bfloat16),
        pltpu.VMEM((n + 1, BLK, 2 * HD), jnp.bfloat16),
        pltpu.SemaphoreType.DMA((n, 3)),
    ]
    out = jax.ShapeDtypeStruct((BLK, HEADS * HD), jnp.bfloat16)
    flops, exps = 6 * (n + HEADS) * BLK * BLK * HD, (n + HEADS) * BLK * BLK
    scalars = (route, place, jnp.asarray(table, jnp.int32))
    return call(attend_kernel, out, scalars, (q, k, v), (*named, *ya), scratch, flops, exps, 56)


def project_own(at, a, w):
    total = jax.ShapeDtypeStruct((BLK, NZ * HD), jnp.float32)
    rows = lambda *n: jax.ShapeDtypeStruct((*n, NZ, BLK, HD), jnp.bfloat16)
    scratch = [pltpu.VMEM((NZ, BLK, HD), jnp.bfloat16), pltpu.SemaphoreType.DMA((4,))]
    return call(own_kernel, (total, rows(2), rows()), (at,), (a,), w, scratch, 2 * BLK * BLK * NZ * HD, vmem=56)


def project_near(total, a0, a1, w):
    out = jax.ShapeDtypeStruct((BLK, NZ * HD), jnp.float32)
    return call(near_kernel, out, (), (total, a0, a1, w), (), (), 4 * BLK * BLK * NZ * HD)


def project_far(core, total, a0, a1, w, dtype):
    out = jax.ShapeDtypeStruct((BLK, NZ * HD // NC), dtype)
    return call(far_kernel, out, (core[None],), (total, a0, a1, w), (), (), 2 * BLK * BLK * NZ * HD // NC)


def body(queries, keys, values, routing, w_out):
    y, z, x, c = (lax.axis_index(a) for a in AXES)
    at = lambda y, z, x, c: ((y * NZ + z) * NX + x) * NC + c
    turn = [
        (at(y, z, x, c), at(x, z, y, c)) for y in range(NY) for z in range(NZ) for x in range(NX) for c in range(NC)
    ]
    route = lax.dynamic_index_in_dim(routing, y * NZ + z, 0, keepdims=False).reshape(-1)

    def rows_of(x):
        d = (x - y) % NX
        return jnp.where(d == 0, 0, jnp.where(d == 3, 1, jnp.where(d == 1, 2, 3)))

    at = jnp.stack([z] + [rows_of(x + d) for d in (0, -1, 1, 2)])
    named, ya, w, (route, at) = gather(jnp.stack([keys, values]).reshape(2 * BLK, HD), w_out, turn, (route, at))
    attn = attention(route, jnp.stack([y, z]), queries, keys, values, named, ya)
    attn, w = gate(attn, w)
    x1p, x1m = xp(attn), xm(attn)
    (x1p, x1m), (total, near, far) = gate((x1p, x1m), project_own(at, attn, w))
    x2p, x2m = xp(x1p[:HALF]), xm(x1m[HALF:])
    total = project_near(total, x1p, x1m, near)
    theirs = swap(project_far(1 - c, total, x2p, x2m, far, jnp.bfloat16))
    mine = project_far(c, total, x2p, x2m, far, jnp.float32)
    return (mine + theirs.astype(jnp.float32)).astype(jnp.bfloat16)


def solution(mesh):
    grid = Mesh(mesh.devices.reshape(NY, NZ, NX, NC), AXES)
    seq, mp = ("y", "z"), ("x", "c")
    in_specs = (P(seq, mp), P(seq, mp), P(seq, mp), P(None, mp, None), P(mp, seq))
    return jax.shard_map(body, mesh=grid, in_specs=in_specs, out_specs=P(seq, mp), check_vma=False)
```

```python
import functools
import math

import jax
import jax.numpy as jnp
from jax import lax
from jax.experimental import pallas as pl
from jax.experimental.pallas import tpu as pltpu
from jax.sharding import Mesh, PartitionSpec as P

HD = 128
BLK = 512
HEADS = 4
SLOTS = 3
NY, NZ, NX, NC = 4, 8, 4, 2
AXES = ("y", "z", "x", "c")
ARRAYS = ("kv", "z1m", "z1p", "z2m", "z2p", "s1m", "s1p", "s2p", "g0p", "g0m")
ARRAYS += ("gap", "gam", "gbp", "gbm", "gcp", "gcm", "gdp")
HALF = BLK // 2
ZROWS = 880
ZVALUES = ZROWS - BLK
LAST = BLK - ZVALUES
SLOT = LAST + BLK
SCALE = math.log2(math.e) / math.sqrt(HD)
def shift(v, axis, d, n):
    return lax.ppermute(v, axis, [(i, (i + d) % n) for i in range(n)])


zp = functools.partial(shift, axis="z", d=1, n=NZ)
zm = functools.partial(shift, axis="z", d=-1, n=NZ)
yp = functools.partial(shift, axis="y", d=1, n=NY)
ym = functools.partial(shift, axis="y", d=-1, n=NY)
y2 = functools.partial(shift, axis="y", d=2, n=NY)
xp = functools.partial(shift, axis="x", d=1, n=NX)
xm = functools.partial(shift, axis="x", d=-1, n=NX)
swap = functools.partial(shift, axis="c", d=1, n=NC)


def gate(vals, waits):
    return lax.optimization_barrier((vals, waits))


def join(*parts):
    return jnp.concatenate(parts)


def places():
    z3 = NY * SLOT
    out = {}
    own = {0: ("kv", 0), 1: ("z1m", 0), 7: ("z1p", 0), 2: ("z2m", 0), 6: ("z2p", 0), 3: ("s1m", z3), 5: ("s1p", z3), 4: ("s2p", z3)}
    side = {0: ("g0", 0), 1: ("ga", 0), 7: ("ga", 1), 2: ("ga", 2), 6: ("ga", 3), 3: ("gb", 0), 5: ("gb", 1), 4: ("gc", 0)}
    far = {0: ("gbm", 2), 1: ("gbp", 2), 7: ("gbp", 3), 2: ("gcp", 1), 6: ("gcm", 1), 3: ("gcp", 2), 5: ("gcm", 2), 4: ("gdp", 0)}
    for dz in range(NZ):
        out[0, dz] = own[dz]
        out[2, dz] = far[dz][0], far[dz][1] * ZROWS
        for dy, way in ((3, "p"), (1, "m")):
            out[dy, dz] = side[dz][0] + way, side[dz][1] * ZROWS
    return out


def gather(kv, w, turn, early):
    half = ZROWS + LAST // 2
    z1p, z1m, g0p, g0m = zp(kv), zm(kv), yp(kv), ym(kv)
    w = lax.ppermute(w, AXES, turn)
    (z1p, z1m, g0p, g0m, w), early = gate((z1p, z1m, g0p, g0m, w), early)
    to_p, to_m, w2, z2p, z2m = join(g0p[ZROWS:half], w), join(g0m[half:], w), y2(w), zp(z1p), zm(z1m)
    both_p, both_m = yp(to_p), ym(to_m)
    (both_p, both_m, w2, z2p, z2m), _ = gate((both_p, both_m, w2, z2p, z2m), ())
    n = LAST // 2
    s0 = kv[ZROWS:], w, g0p[ZROWS:], both_p[n:], g0m[ZROWS:], both_m[n:], both_p[:n], both_m[:n], w2
    s0p, s0m, ga = join(*s0, z2p[:ZROWS]), join(*s0, z2m[:ZROWS]), join(*(v[:ZROWS] for v in (z1m, z1p, z2m, z2p)))
    s1p, s1m, gap, gam = zp(s0p), zm(s0m), yp(ga), ym(ga)
    (s1p, s1m, gap, gam), _ = gate((s1p, s1m, gap, gam), ())
    z3, chunk = NY * SLOT, lambda v, i: v[i * ZROWS : (i + 1) * ZROWS]
    z3m, z3p = s1m[z3:], s1p[z3:]
    s2p, s2m, gbp, gbm = zp(s1p), zm(s1m), yp(join(z3m, z3p, gap[: 2 * ZROWS])), ym(join(z3m, z3p, g0m[:ZROWS]))
    (s2p, s2m, gbp, gbm), _ = gate((s2p, s2m, gbp, gbm), ())
    z4 = s2p[z3:]
    s3p, s3m = zp(s2p[:z3]), zm(s2m[:z3])
    gcp, gcm = yp(join(z4, chunk(gap, 2), chunk(gbp, 0))), ym(join(z4, chunk(gam, 3), chunk(gbm, 1)))
    (s3p, s3m, gcp, gcm), _ = gate((s3p, s3m, gcp, gcm), ())
    s4p, s4m, gdp = zp(s3p[: z3 // 2]), zm(s3m[z3 // 2 :]), yp(chunk(gcp, 0))
    named = (kv, z1m, z1p, z2m, z2p, s1m, s1p, s2p, g0p, g0m, gap, gam, gbp, gbm, gcp, gcm, gdp)
    return named, [s0p, s1m, s2m, s3m, s4p, s3p, s2p, s1p, s4m], early


TILE = 128


def attend_kernel(route_ref, place_ref, table_ref, q_ref, k_ref, v_ref, *rest):
    count = len(ARRAYS)
    named, ya, out_ref, (kbuf, vbuf, sems) = rest[:count], rest[count : count + 9], rest[count + 9], rest[count + 10 :]
    n = HEADS * SLOTS
    y, z = place_ref[0], place_ref[1]
    me = y * NZ + z

    def copies(u, i, block, first):
        rows = lambda at, size: block.at[pl.ds(pl.multiple_of(first + at, 16), size)]
        part = lambda at, size: vbuf.at[u, pl.ds(at, size), pl.ds(0, HD)]
        if i == 1:
            return [pltpu.make_async_copy(rows(0, LAST), part(ZVALUES, LAST), sems.at[u, 2])]
        return [
            pltpu.make_async_copy(rows(0, BLK), kbuf.at[u], sems.at[u, 0]),
            pltpu.make_async_copy(rows(BLK, ZVALUES), part(0, ZVALUES), sems.at[u, 1]),
        ]

    def start(u, i, arrays, array, first, step):
        for low in range(0, len(arrays), step):

            @pl.when((array >= low) & (array < low + step))
            def _():
                for a in range(low, min(low + step, len(arrays))):

                    @pl.when(array == a)
                    def _():
                        for copy in copies(u, i, arrays[a], first):
                            copy.start()

    for u in range(n):
        j = route_ref[u]
        by, dz = j >> 3, (j - z) & (NZ - 1)
        dy = (by - y) & (NY - 1)
        code = table_ref[dy * NZ + dz]
        start(u, 0, named, code & 31, (code >> 5) * 16, 5)
        slot = jnp.where(dy == 0, 0, jnp.where(dy == 3, 1, jnp.where(dy == 1, 2, 3)))
        late = (dz == 4) & (slot >= 2)
        start(u, 1, ya, jnp.where(late, NZ, dz), jnp.where(late, slot - 2, slot) * SLOT, 3)

    for u in range(n + 1):
        vbuf[u, :, HD:] = jnp.ones((BLK, HD), jnp.bfloat16)
    vbuf[n, :, :HD] = v_ref[...]
    scores_of = lambda q, k: lax.dot_general(q, k, (((1,), (1,)), ((), ())), preferred_element_type=jnp.float32)
    for h in range(HEADS):
        cols = slice(h * HD, (h + 1) * HD)
        for s in range(SLOTS):
            u = h * SLOTS + s
            for i, arrays in enumerate((named, ya)):
                for copy in copies(u, i, arrays[0], 0):
                    copy.wait()
        for t in range(BLK // TILE):
            rows = slice(t * TILE, (t + 1) * TILE)
            q = q_ref[rows, cols]
            seen = (t + 1) * TILE
            own = scores_of(q, k_ref[:seen])
            later = lax.broadcasted_iota(jnp.int32, (TILE, seen), 1) - t * TILE
            own = jnp.where(lax.broadcasted_iota(jnp.int32, (TILE, seen), 0) >= later, own, -1e30)
            m = jnp.max(own, axis=1, keepdims=True) * SCALE
            scores = []
            for s in range(SLOTS):
                u = h * SLOTS + s
                sc = scores_of(q, kbuf[u])
                top = jnp.max(sc, axis=1, keepdims=True) * SCALE
                m = jnp.maximum(m, jnp.where(route_ref[u] < me, top, -1e30))
                scores.append(sc)
            e = jnp.exp2(own * SCALE - m).astype(jnp.bfloat16)
            both = jnp.dot(e, vbuf[n, :seen], preferred_element_type=jnp.float32)
            for s in range(SLOTS):
                u = h * SLOTS + s
                e = jnp.exp2(scores[s] * SCALE - jnp.where(route_ref[u] < me, m, 1e30)).astype(jnp.bfloat16)
                both = both + jnp.dot(e, vbuf[u], preferred_element_type=jnp.float32)
            out_ref[rows, cols] = (both[:, :HD] / both[:, HD:]).astype(out_ref.dtype)


def own_kernel(at_ref, a_ref, *rest):
    arrays, total_ref, near_ref, far_ref, buf, sems = rest[:9], rest[9], rest[10], rest[11], rest[12], rest[13]
    dests = (buf, near_ref.at[0], near_ref.at[1], far_ref)
    for i, dest in enumerate(dests):
        slot = at_ref[1 + i]
        for dz in range(NZ):
            col = (at_ref[0] + dz) & (NZ - 1)

            def copy(array, at):
                rows = pl.ds(pl.multiple_of(at * SLOT + LAST, 16), BLK)
                pltpu.make_async_copy(array.at[rows], dest.at[col], sems.at[i]).start()

            if dz == 4:
                pl.when(slot < 2)(lambda: copy(arrays[4], slot))
                pl.when(slot >= 2)(lambda: copy(arrays[8], slot - 2))
            else:
                copy(arrays[dz], slot)
    pltpu.make_async_copy(buf, buf, sems.at[0]).wait()
    for n in range(NZ // 2):
        cols = jnp.concatenate([buf[2 * n], buf[2 * n + 1]], axis=1)
        total_ref[:, n * 2 * HD : (n + 1) * 2 * HD] = jnp.dot(a_ref[...], cols, preferred_element_type=jnp.float32)
    for i, dest in enumerate(dests[1:]):
        pltpu.make_async_copy(dest, dest, sems.at[1 + i]).wait()


def near_kernel(total_ref, a0_ref, a1_ref, w_ref, out_ref):
    for n in range(NZ // 2):
        cols = slice(n * 2 * HD, (n + 1) * 2 * HD)
        total = total_ref[:, cols]
        for i, a_ref in enumerate((a0_ref, a1_ref)):
            rows = jnp.concatenate([w_ref[i, 2 * n], w_ref[i, 2 * n + 1]], axis=1)
            total = total + jnp.dot(a_ref[...], rows, preferred_element_type=jnp.float32)
        out_ref[:, cols] = total


def far_kernel(core_ref, total_ref, a0_ref, a1_ref, w_ref, out_ref):
    width, count = NZ * HD // NC, NZ // NC
    core = core_ref[0]
    for i, a_ref in enumerate((a0_ref, a1_ref)):
        rows = slice(i * HALF, (i + 1) * HALF)
        for n in range(count // 2):
            right = jnp.concatenate([w_ref[core * count + 2 * n], w_ref[core * count + 2 * n + 1]], axis=1)
            part = jnp.dot(a_ref[...], right, preferred_element_type=jnp.float32)
            cols = pl.ds(pl.multiple_of(core * width, width) + n * 2 * HD, 2 * HD)
            out_ref[rows, n * 2 * HD : (n + 1) * 2 * HD] = (total_ref[rows, cols] + part).astype(out_ref.dtype)


def call(kernel, out_shape, scalars, near, far, scratch, flops, exps=0, vmem=32):
    spec = lambda space, arrays: [pl.BlockSpec(memory_space=space)] * len(arrays)
    return pl.pallas_call(
        kernel,
        out_shape=out_shape,
        in_specs=spec(pltpu.SMEM, scalars) + spec(pltpu.VMEM, near) + spec(pl.ANY, far),
        out_specs=jax.tree.map(lambda _: pl.BlockSpec(memory_space=pltpu.VMEM), out_shape),
        scratch_shapes=scratch,
        compiler_params=pltpu.CompilerParams(vmem_limit_bytes=vmem << 20),
        cost_estimate=pl.CostEstimate(flops=flops, transcendentals=exps, bytes_accessed=8 << 20),
    )(*scalars, *near, *far)


def attention(route, place, q, k, v, named, ya):
    n = HEADS * SLOTS
    table = [0] * (NY * NZ)
    for (dy, dz), (name, first) in places().items():
        table[dy * NZ + dz] = ARRAYS.index(name) + first // 16 * 32
    scratch = [
        pltpu.VMEM((n, BLK, HD), jnp.bfloat16),
        pltpu.VMEM((n + 1, BLK, 2 * HD), jnp.bfloat16),
        pltpu.SemaphoreType.DMA((n, 3)),
    ]
    out = jax.ShapeDtypeStruct((BLK, HEADS * HD), jnp.bfloat16)
    flops, exps = 6 * (n + HEADS) * BLK * BLK * HD, (n + HEADS) * BLK * BLK
    scalars = (route, place, jnp.asarray(table, jnp.int32))
    return call(attend_kernel, out, scalars, (q, k, v), (*named, *ya), scratch, flops, exps, 56)


def project_own(at, a, w):
    total = jax.ShapeDtypeStruct((BLK, NZ * HD), jnp.float32)
    rows = lambda *n: jax.ShapeDtypeStruct((*n, NZ, BLK, HD), jnp.bfloat16)
    scratch = [pltpu.VMEM((NZ, BLK, HD), jnp.bfloat16), pltpu.SemaphoreType.DMA((4,))]
    return call(own_kernel, (total, rows(2), rows()), (at,), (a,), w, scratch, 2 * BLK * BLK * NZ * HD, vmem=56)


def project_near(total, a0, a1, w):
    out = jax.ShapeDtypeStruct((BLK, NZ * HD), jnp.float32)
    return call(near_kernel, out, (), (total, a0, a1, w), (), (), 4 * BLK * BLK * NZ * HD)


def project_far(core, total, a0, a1, w, dtype):
    out = jax.ShapeDtypeStruct((BLK, NZ * HD // NC), dtype)
    return call(far_kernel, out, (core[None],), (total, a0, a1, w), (), (), 2 * BLK * BLK * NZ * HD // NC)


def body(queries, keys, values, routing, w_out):
    y, z, x, c = (lax.axis_index(a) for a in AXES)
    at = lambda y, z, x, c: ((y * NZ + z) * NX + x) * NC + c
    turn = [
        (at(y, z, x, c), at(x, z, y, c)) for y in range(NY) for z in range(NZ) for x in range(NX) for c in range(NC)
    ]
    route = lax.dynamic_index_in_dim(routing, y * NZ + z, 0, keepdims=False).reshape(-1)

    def rows_of(x):
        d = (x - y) % NX
        return jnp.where(d == 0, 0, jnp.where(d == 3, 1, jnp.where(d == 1, 2, 3)))

    at = jnp.stack([z] + [rows_of(x + d) for d in (0, -1, 1, 2)])
    named, ya, (route, at) = gather(jnp.stack([keys, values]).reshape(2 * BLK, HD), w_out, turn, (route, at))
    attn = attention(route, jnp.stack([y, z]), queries, keys, values, named, ya)
    x1p, x1m = xp(attn), xm(attn)
    (x1p, x1m), (total, near, far) = gate((x1p, x1m), project_own(at, attn, ya))
    x2p, x2m = xp(x1p[:HALF]), xm(x1m[HALF:])
    total = project_near(total, x1p, x1m, near)
    theirs = swap(project_far(1 - c, total, x2p, x2m, far, jnp.bfloat16))
    mine = project_far(c, total, x2p, x2m, far, jnp.float32)
    return (mine + theirs.astype(jnp.float32)).astype(jnp.bfloat16)


def solution(mesh):
    grid = Mesh(mesh.devices.reshape(NY, NZ, NX, NC), AXES)
    seq, mp = ("y", "z"), ("x", "c")
    in_specs = (P(seq, mp), P(seq, mp), P(seq, mp), P(None, mp, None), P(mp, seq))
    return jax.shard_map(body, mesh=grid, in_specs=in_specs, out_specs=P(seq, mp), check_vma=False)
```
